256 devices in a mesh: dp: 16 (over z, core), expert: 16 (over y, x).
Axes of the slice: x: 4, y: 4, z: 8, core: 2. Of those that a mesh axis runs over, the one named last changes fastest.
Arguments:
- tokens: bfloat16 [2048, 4096], P('expert', 'dp'), may hold values from -6 to 6
- cotangent: bfloat16 [2048, 4096], P('expert', 'dp'), may hold values from -6 to 6
- routing: int32 [2048, 8], P('expert'), may hold values from 0 to 63, all different within a row; in each aligned block of 128 rows (0 to 127, 128 to 255, ...) at most 24 rows name the same one
- w_router: bfloat16 [4096, 64], P('dp'), may hold values from -0.7 to 0.7
- running_mean: bfloat16 [64, 4096], P(None, 'dp'), may hold values from -3 to 3
- w_gate: bfloat16 [64, 4096, 768], P('expert', 'dp'), may hold values from -0.09375 to 0.09375
- w_up: bfloat16 [64, 4096, 768], P('expert', 'dp'), may hold values from -0.09375 to 0.09375
- w_down: bfloat16 [64, 768, 4096], P('expert', None, 'dp'), may hold values from -0.21875 to 0.21875
Outputs:
- grad_tokens: bfloat16 [2048, 4096], P('expert', 'dp')
- grad_router: float32 [4096, 64], P('dp')
- grad_gate: bfloat16 [64, 4096, 768], P('expert', 'dp')
- grad_up: bfloat16 [64, 4096, 768], P('expert', 'dp')
- grad_down: bfloat16 [64, 768, 4096], P('expert', None, 'dp')
The draws below stay inside these ranges and needn't reach their ends.
Inputs may be any that keep to these rules, and one draw needn't show every extreme that they name: `routing`: each row names 8 different experts. In each aligned block of 128 tokens no expert is named by more than 24 tokens, a bound that some block reaches.
All inputs are finite; a program needn't handle non-finite values.
Results may differ from the reference program's by a relative error of at most 0.035.
Values may be sent and summed in bfloat16 or wider, within the bound.
A program may use at most 192 MiB of HBM per device.

```python
import math
import jax
import jax.numpy as jnp
import numpy as np
from jax import lax

D = 4096
H = 768
TOP = 8
TOK_DEV = 128
EXPERTS = 64
TOKENS = 2048
CAP = 24
DSLICE = 256
N_DP = 16
N_EXPERT = 16


def draw_tokens(key, part):
    key = jax.random.fold_in(key, 3)
    noise = jax.random.truncated_normal(key, -6.0, 6.0, (TOKENS, D), jnp.float32)
    return noise.astype(jnp.bfloat16)


def draw_w_router(key, part):
    key = jax.random.fold_in(key, 5)
    spread = 0.5 / math.sqrt(D)
    noise = jax.random.truncated_normal(key, -4.0, 4.0, (D, EXPERTS), jnp.float32)
    return (spread * noise).astype(jnp.bfloat16)


def block_levels(rng, extent, cuts, least, top_value):
    def one(axis_at, shards_of):
        heights = jax.random.uniform(jax.random.fold_in(jax.random.fold_in(rng, 6), axis_at), (shards_of,), jnp.float32, least / len(cuts), top_value / len(cuts))
        return jnp.repeat(jnp.exp(heights), extent[axis_at] // shards_of).reshape((-1,) + (1,) * (len(extent) - axis_at - 1))

    loudness = one(*cuts[0])
    for cut in cuts[1:]:
        loudness = loudness * one(*cut)
    return loudness


def routed_block(rng, own, number, rows, number_of, top, limit, skew):
    ranking = jax.random.permutation(rng, number_of)
    heavy_load, common = load_shares(number_of, rows * top, limit, skew, True), load_shares(number_of, rows * top, limit, skew, False)
    places = jnp.arange(number_of)

    def named(lengths, rotation):
        used = int((lengths > 0).sum())
        fixed = max(1, used // 4)
        moved = fixed + (places - fixed + rotation * (used - fixed)) % max(1, number_of - fixed)
        return jnp.zeros((number_of,), jnp.int32).at[ranking[jnp.where(places < fixed, places, moved)]].set(jnp.asarray(lengths, jnp.int32))

    lengths = jnp.where(number % 4 == 0, named(heavy_load, number // 4), named(common, number - number // 4 - 1))
    mixed = jax.random.permutation(jax.random.fold_in(own, 3), number_of)
    source_of, sink = mixed[0:number_of // 2 * 2:2], mixed[1:number_of // 2 * 2:2]
    slack = jnp.minimum(lengths[source_of] - 1, limit - lengths[sink]) // 2
    slack = jnp.where((source_of == ranking[0]) | (sink == ranking[0]) | (lengths[sink] == 0), 0, jnp.maximum(slack, 0))
    moved = jax.random.randint(jax.random.fold_in(own, 4), (number_of // 2,), 0, 1 << 20) % (slack + 1)
    lengths = lengths.at[source_of].add(-moved).at[sink].add(moved)
    items = jnp.searchsorted(jnp.cumsum(lengths), jnp.arange(rows * top), side="right").astype(jnp.int32)
    table = items.reshape(top, rows).T
    table = table[jax.random.permutation(jax.random.fold_in(own, 1), rows)]
    rotation = jax.random.randint(jax.random.fold_in(own, 2), (rows, 1), 0, top)
    return jnp.take_along_axis(table, (jnp.arange(top)[None, :] + rotation) % top, axis=1)


def load_shares(count, total, most, lean, full):
    loads = [(1 << 20) // math.isqrt(grade ** lean) + 1 for grade in range(1, count + 1)]
    largest = most if full else min(most, max(-(-total // count), total * loads[0] // sum(loads)))
    least = 1 if total - largest >= count - 1 else 0
    holding, rest = [largest] + [least] * (count - 1), total - largest - least * (count - 1)
    while rest > 0:
        free = [i for i in range(1, count) if holding[i] < largest] or [i for i in range(1, count) if holding[i] < most]
        mass, remaining = sum([loads[i] for i in free]), rest
        for i in free:
            extra = min(most - holding[i], max(1, remaining * loads[i] // mass), rest)
            holding[i] = holding[i] + extra
            rest = rest - extra
    return np.array(holding)


def bell_draw(own_key, extent, deviation, most, pieces=(), kind=jnp.bfloat16):
    array = jax.random.normal(own_key, extent, jnp.float32) * deviation
    if len(pieces) > 0:
        array = block_levels(own_key, extent, pieces, -0.22, 0.18) * array
    return jnp.clip(array, min=-most, max=most).astype(kind)


def setup_inputs(seed: int = 0) -> dict:
    arg_keys = jax.random.split(jax.random.key(seed), 9)
    tokens = draw_tokens(jax.random.fold_in(arg_keys[8], 71), 0)
    cotangent = bell_draw(arg_keys[1], (TOKENS, D), 1.0, 6.0, ((0, 16), (1, 16)))
    routing_keys = jax.random.split(jax.random.fold_in(arg_keys[2], 1), TOKENS // TOK_DEV)
    routing_turns = jax.random.permutation(jax.random.fold_in(arg_keys[2], 3), TOKENS // TOK_DEV)
    routing = jax.vmap(lambda own, number: routed_block(jax.random.fold_in(arg_keys[2], 2), own, number, TOK_DEV, EXPERTS, TOP, CAP, 2))(routing_keys, routing_turns).reshape((TOKENS, TOP))
    w_router = draw_w_router(jax.random.fold_in(arg_keys[8], 71), 0)
    running_mean = bell_draw(arg_keys[4], (EXPERTS, D), 0.5, 3.0, ((1, 16),))
    w_gate = bell_draw(arg_keys[5], (EXPERTS, D, H), D ** -0.5, 0.09375, ((0, 16), (1, 16)))
    w_up = bell_draw(arg_keys[6], (EXPERTS, D, H), D ** -0.5, 0.09375, ((0, 16), (1, 16)))
    w_down = bell_draw(arg_keys[7], (EXPERTS, H, D), H ** -0.5, 0.21875, ((0, 16), (2, 16)))
    return {"tokens": tokens, "cotangent": cotangent, "routing": routing, "w_router": w_router, "running_mean": running_mean, "w_gate": w_gate, "w_up": w_up, "w_down": w_down}


def rounded(value):
    return lax.optimization_barrier(value.astype(jnp.bfloat16)).astype(jnp.float32)


def blocked_forward(left, weight):
    count = left.shape[0]
    parts = jnp.einsum("rbd,bdh->rbh", left.reshape(count, N_DP, DSLICE).astype(jnp.float32), weight.reshape(N_DP, DSLICE, H).astype(jnp.float32))
    return jnp.sum(rounded(parts), axis=1)


def blocked_backward(left, weight):
    count = left.shape[0]
    parts = jnp.einsum("rbd,hbd->rbh", left.reshape(count, N_DP, DSLICE).astype(jnp.float32), weight.reshape(H, N_DP, DSLICE).astype(jnp.float32))
    return jnp.sum(rounded(parts), axis=1)


def reference(tokens, cotangent, routing, w_router, running_mean, w_gate, w_up, w_down):
    logits = jnp.dot(tokens, w_router, preferred_element_type=jnp.float32)
    weights_exp = jnp.exp(logits)
    router_prob = weights_exp / jnp.sum(weights_exp, axis=1, keepdims=True)
    pair_count = TOKENS * TOP
    flat_route = routing.reshape(-1).astype(jnp.int32)
    onehot = (flat_route[:, None] == jnp.arange(EXPERTS, dtype=jnp.int32)[None, :]).astype(jnp.int32)
    blocked = onehot.reshape(N_EXPERT, TOK_DEV * TOP, EXPERTS)
    before = (jnp.cumsum(blocked, axis=1) - blocked).reshape(pair_count, EXPERTS)
    position = jnp.sum(before * onehot, axis=1).astype(jnp.int32)
    pair_token = (jnp.arange(pair_count, dtype=jnp.int32) // TOP).astype(jnp.int32)
    row_index = ((pair_token // TOK_DEV) * CAP + position).astype(jnp.int32)
    row_total = N_EXPERT * CAP
    table = jnp.full((EXPERTS, row_total), -1, jnp.int32).at[flat_route, row_index].set(pair_token)
    valid = table >= 0
    safe_table = jnp.maximum(table, 0)
    pair_prob = router_prob[pair_token, flat_route].astype(jnp.bfloat16)
    slot_prob = jnp.zeros((EXPERTS, row_total), jnp.bfloat16).at[flat_route, row_index].set(pair_prob)

    def expert_step(index):
        slot_rows = safe_table[index]
        alive_rows = valid[index][:, None]
        slot_tokens = jnp.where(alive_rows, tokens[slot_rows], jnp.zeros((), jnp.bfloat16))
        slot_grads = jnp.where(alive_rows, cotangent[slot_rows], jnp.zeros((), jnp.bfloat16))
        gate_weight = w_gate[index]
        up_weight = w_up[index]
        down_weight = w_down[index]
        gate_value = blocked_forward(slot_tokens, gate_weight)
        up_value = blocked_forward(slot_tokens, up_weight)
        sigmoid_gate = jax.nn.sigmoid(gate_value)
        silu_gate = gate_value * sigmoid_gate
        hidden_act = (silu_gate * up_value).astype(jnp.bfloat16)
        expert_out = jnp.dot(hidden_act, down_weight, preferred_element_type=jnp.float32)
        grads_float = slot_grads.astype(jnp.float32)
        slot_dots = jnp.sum((expert_out * grads_float).reshape(row_total, N_DP, DSLICE), axis=2).astype(jnp.bfloat16)
        scaled = (slot_prob[index].astype(jnp.float32)[:, None] * grads_float).astype(jnp.bfloat16)
        d_hidden = blocked_backward(scaled, down_weight)
        d_gate = (d_hidden * up_value * sigmoid_gate * (1.0 + gate_value * (1.0 - sigmoid_gate))).astype(jnp.bfloat16)
        d_up = (d_hidden * silu_gate).astype(jnp.bfloat16)
        dx_slots = (jnp.dot(d_gate, gate_weight.T, preferred_element_type=jnp.float32) + jnp.dot(d_up, up_weight.T, preferred_element_type=jnp.float32)).astype(jnp.bfloat16)
        grad_gate = jnp.dot(slot_tokens.T, d_gate, preferred_element_type=jnp.float32).astype(jnp.bfloat16)
        grad_up = jnp.dot(slot_tokens.T, d_up, preferred_element_type=jnp.float32).astype(jnp.bfloat16)
        grad_down = jnp.dot(hidden_act.T, scaled, preferred_element_type=jnp.float32).astype(jnp.bfloat16)
        return dx_slots, slot_dots, grad_gate, grad_up, grad_down

    dx_slots, slot_dots, grad_gate, grad_up, grad_down = lax.map(expert_step, jnp.arange(EXPERTS, dtype=jnp.int32))
    flat_valid = valid.reshape(-1)
    flat_rows = safe_table.reshape(-1)
    dx_values = jnp.where(flat_valid[:, None], dx_slots.reshape(-1, D).astype(jnp.float32), jnp.zeros((), jnp.float32))
    dx_experts = jnp.zeros((TOKENS, D), jnp.float32).at[flat_rows].add(dx_values)
    dots_total = jnp.sum(slot_dots.astype(jnp.float32), axis=2).reshape(-1)
    expert_ids = jnp.repeat(jnp.arange(EXPERTS, dtype=jnp.int32), row_total)
    top_dense = jnp.zeros((TOKENS, EXPERTS), jnp.float32).at[flat_rows, expert_ids].add(jnp.where(flat_valid, dots_total, jnp.zeros((), jnp.float32)))
    chosen = jnp.zeros((TOKENS, EXPERTS), jnp.int32).at[pair_token, flat_route].set(1) > 0
    mean_dots = jnp.dot(cotangent, running_mean.T, preferred_element_type=jnp.float32)
    d_prob = jnp.where(chosen, top_dense, mean_dots)
    dlogits = router_prob * (d_prob - jnp.sum(router_prob * d_prob, axis=1, keepdims=True))
    grad_router = jnp.dot(tokens.astype(jnp.float32).T, dlogits, precision=lax.Precision.HIGHEST)
    router_term = jnp.dot(dlogits, w_router.astype(jnp.float32).T, precision=lax.Precision.HIGHEST)
    grad_tokens = (dx_experts + router_term).astype(jnp.bfloat16)
    return grad_tokens, grad_router, grad_gate, grad_up, grad_down
```

```python
import functools

import jax
import jax.numpy as jnp
from jax import lax
from jax.experimental import pallas as pl
from jax.experimental.pallas import tpu as pltpu
from jax.sharding import PartitionSpec as P

MESH = pl.DeviceIdType.MESH
BF = jnp.bfloat16
F32 = jnp.float32
CORES = 2
RS_LAG = 2
AG_LAG = 3


def rem(a, n):
    return lax.rem(a, jnp.int32(n))


def div(a, n):
    return lax.div(a, jnp.int32(n))


def remote(src, dst, send_sem, recv_sem, device):
    return pltpu.make_async_remote_copy(
        src_ref=src,
        dst_ref=dst,
        send_sem=send_sem,
        recv_sem=recv_sem,
        device_id=device,
        device_id_type=MESH,
    )


def loop(lower, upper, body):
    def step(i, carry):
        body(i)
        return carry

    lax.fori_loop(lower, upper, step, 0)


def dot_nn(a, b):
    return jnp.dot(a, b, preferred_element_type=F32)


def dot_nt(a, b):
    return lax.dot_general(a, b, (((1,), (1,)), ((), ())), preferred_element_type=F32)


def dot_tn(a, b):
    return lax.dot_general(a, b, (((0,), (0,)), ((), ())), preferred_element_type=F32)


def split_two(value):
    high = value.astype(BF)
    low = (value - high.astype(F32)).astype(BF)
    return high, low


def kernel(
    sizes,
    tokens, cotangent, routing, w_router, running_mean, w_gate, w_up, w_down,
    grad_tokens, grad_router, grad_gate, grad_up, grad_down,
    place, send_rows, in_rows, rows, wg, wu, wd,
    part, recv, full,
    sum_src, sum_in, sum_out, gr_src, gr_in, gr_out,
    prob_ref, w_send, w_in, dots_send, dots_in, top_send, top_in, dlog_hi, dlog_lo,
    dx_ref, back_send, back_in, out_gate, out_up, out_down,
    rows_s, rows_r, wx_s, wx_r, wl_s,
    p1_s, p1_r, p2_s, p2_r,
    rs_s, rs_r, ag_s, ag_r,
    wt_s, wt_r, dt_s, dt_r, tp_s, tp_r, bk_s, bk_r,
    ol_s, ox_s, ox_r,
):
    NE, Z, E, TOK, H, W, CAP = sizes
    ND = Z * CORES
    NQ = NE * CORES
    S = NE // Z
    HH = H // 2
    EL = 64
    PAIR = 2 * CAP
    ROWS = NE * CAP

    dp = lax.axis_index("dp")
    xy = lax.axis_index("expert")
    z = div(dp, CORES)
    c = rem(dp, CORES)
    other = 1 - c
    q = xy * CORES + c
    right = rem(z + 1, Z)
    left = rem(z + Z - 1, Z)
    twin = (z * CORES + other, xy)

    def plane_peer(q2):
        return (z * CORES + rem(q2, CORES), div(q2, CORES))

    barrier = pltpu.get_barrier_semaphore()

    def greet_plane(k):
        pl.semaphore_signal(
            barrier, inc=1, device_id=plane_peer(rem(q + k, NQ)), device_id_type=MESH
        )

    def greet_column(m):
        z2 = rem(z + 1 + div(m, CORES), Z)
        pl.semaphore_signal(
            barrier, inc=1, device_id=(z2 * CORES + rem(m, CORES), xy), device_id_type=MESH
        )

    loop(1, NQ, greet_plane)
    loop(0, CORES * (Z - 1), greet_column)

    def own_weights(i, src, dst):
        return pltpu.make_async_copy(src, dst, wl_s.at[i])

    half = pl.ds(pl.multiple_of(c * W, W), W)
    mine = pl.ds(c * 2, 2)
    theirs = pl.ds(other * 2, 2)
    own_copies = [
        own_weights(0, w_gate.at[mine], wg.at[:, half, :]),
        own_weights(1, w_up.at[mine], wu.at[:, half, :]),
        own_weights(2, w_down.at[mine], wd.at[c]),
    ]
    for copy in own_copies:
        copy.start()

    route = routing[...]
    lane = lax.broadcasted_iota(jnp.int32, (TOK, E), 1)
    chosen = jnp.zeros((TOK, E), F32)
    for k in range(route.shape[1]):
        chosen = chosen + jnp.where(route[:, k : k + 1] == lane, 1.0, 0.0)
    chosen_b = chosen.astype(BF)
    t_row = lax.broadcasted_iota(jnp.int32, (TOK, TOK), 0)
    t_col = lax.broadcasted_iota(jnp.int32, (TOK, TOK), 1)
    before = jnp.where(t_row < t_col, 1.0, 0.0).astype(BF)
    same = jnp.where(t_row == t_col, 1.0, 0.0).astype(BF)
    pos = dot_tn(chosen_b, before)
    has = dot_tn(chosen_b, same)
    pos = jnp.where(has > 0.5, pos, -1.0)
    slot_iota = lax.broadcasted_iota(jnp.int32, (E, CAP, TOK), 1).astype(F32)
    placing = jnp.where(pos[:, None, :] == slot_iota, 1.0, 0.0)
    placing = placing.reshape(E * CAP, TOK).astype(BF)
    place[...] = placing.reshape(NE, CORES, PAIR, TOK)
    send_rows[0] = dot_nn(placing, tokens[...]).astype(BF).reshape(NQ, PAIR, W)
    send_rows[1] = dot_nn(placing, cotangent[...]).astype(BF).reshape(NQ, PAIR, W)

    pl.semaphore_wait(barrier, NQ - 1 + CORES * (Z - 1))

    def rows_copy(which, q2):
        return remote(
            send_rows.at[which, q2], in_rows.at[which, c, xy],
            rows_s.at[which, q2], rows_r.at[which, q], plane_peer(q2),
        )

    def rows_arrival(which, q2):
        return remote(
            send_rows.at[which, q2], in_rows.at[which, rem(q2, CORES), div(q2, CORES)],
            rows_s.at[which, q2], rows_r.at[which, q2], plane_peer(q2),
        )

    weight_copies = [
        remote(w_gate.at[theirs], wg.at[:, half, :], wx_s.at[0], wx_r.at[0], twin),
        remote(w_up.at[theirs], wu.at[:, half, :], wx_s.at[1], wx_r.at[1], twin),
        remote(w_down.at[theirs], wd.at[c], wx_s.at[2], wx_r.at[2], twin),
    ]
    other_half = pl.ds(pl.multiple_of(other * W, W), W)
    weight_arrivals = [
        remote(w_gate.at[theirs], wg.at[:, other_half, :], wx_s.at[0], wx_r.at[0], twin),
        remote(w_up.at[theirs], wu.at[:, other_half, :], wx_s.at[1], wx_r.at[1], twin),
        remote(w_down.at[theirs], wd.at[other], wx_s.at[2], wx_r.at[2], twin),
    ]
    weight_copies[0].start()
    weight_copies[1].start()
    loop(1, NQ, lambda k: rows_copy(0, rem(q + k, NQ)).start())
    loop(1, NQ, lambda k: rows_copy(1, rem(q + k, NQ)).start())
    weight_copies[2].start()
    in_rows[0, c, xy] = send_rows[0, q]
    in_rows[1, c, xy] = send_rows[1, q]

    def sum_blocks(n, index, peer, src, into, out, sem_s, sem_r):
        def scatter(j):
            return remote(src.at[j], into.at[index], sem_s.at[0, j], sem_r.at[0, index], peer(j))

        def scatter_arrival(j):
            return remote(src.at[j], into.at[j], sem_s.at[0, j], sem_r.at[0, j], peer(j))

        def gather(j):
            return remote(
                out.at[index], out.at[index], sem_s.at[1, j], sem_r.at[1, index], peer(j)
            )

        def gather_arrival(j):
            return remote(out.at[j], out.at[j], sem_s.at[1, j], sem_r.at[1, j], peer(j))

        def send():
            loop(1, n, lambda k: scatter(rem(index + k, n)).start())
            into[index] = src[index]

        def reduce():
            loop(1, n, lambda k: scatter_arrival(rem(index + k, n)).wait_recv())
            out[index] = jnp.sum(into[...], axis=0)
            loop(1, n, lambda k: gather(rem(index + k, n)).start())

        def finish():
            loop(1, n, lambda k: gather_arrival(rem(index + k, n)).wait_recv())

        def drain():
            loop(1, n, lambda k: scatter(rem(index + k, n)).wait_send())
            loop(1, n, lambda k: gather(rem(index + k, n)).wait_send())

        return send, reduce, finish, drain

    p1_send, p1_reduce, p1_finish, p1_drain = sum_blocks(
        ND, dp, lambda j: (j, xy), sum_src, sum_in, sum_out, p1_s, p1_r
    )
    p2_send, p2_reduce, p2_finish, p2_drain = sum_blocks(
        NE, xy, lambda j: (dp, j), gr_src, gr_in, gr_out, p2_s, p2_r
    )

    def packed(first, second, count):
        if E < EL:
            gap = jnp.zeros((TOK, EL - E), F32)
            first = jnp.concatenate([first, gap], axis=1)
            second = jnp.concatenate([second, gap], axis=1)
        return jnp.concatenate([first, second], axis=1).reshape(count, TOK // count, 2 * EL)

    logits_part = dot_nn(tokens[...], w_router[...])
    mean_part = dot_nt(cotangent[...], running_mean[...])
    sum_src[...] = packed(logits_part, mean_part, ND)
    p1_send()

    def order_rows(which):
        def body(p):
            for h in range(CORES):
                block = in_rows[which, h, pl.ds(p * 2, 2)].astype(F32)
                for j in range(2):
                    piece = block[:, j * CAP : (j + 1) * CAP, :].reshape(PAIR, W)
                    rows[
                        which, j, pl.ds(pl.multiple_of(p * PAIR, PAIR), PAIR), h * W : (h + 1) * W
                    ] = piece.astype(BF)

        loop(0, NE // 2, body)

    def rs_copy(k, r, s):
        t = rem(z - 1 - s + 2 * Z, Z) if r == 0 else rem(z + 1 + s, Z)
        peer = ((right if r == 0 else left) * CORES + c, xy)
        return remote(
            part.at[k, r, t], recv.at[k, r, s], rs_s.at[k, r, s], rs_r.at[k, r, s], peer
        )

    def rs_step(k, r, s):
        rs_copy(k, r, s).wait_recv()
        t = rem(z - 2 - s + 2 * Z, Z) if r == 0 else rem(z + 2 + s, Z)
        part[k, r, t] = (part[k, r, t].astype(F32) + recv[k, r, s].astype(F32)).astype(BF)
        rs_copy(k, r, s + 1).start()

    def ag_copy(k, r, s):
        t = rem(z - s + Z, Z) if r == 0 else rem(z + s, Z)
        peer = ((right if r == 0 else left) * CORES + c, xy)
        return remote(
            full.at[k, r, t], full.at[k, r, t], ag_s.at[k, r, s], ag_r.at[k, r, s], peer
        )

    def ag_arrival(k, r, s):
        t = rem(z - 1 - s + Z, Z) if r == 0 else rem(z + 1 + s, Z)
        peer = ((right if r == 0 else left) * CORES + c, xy)
        return remote(
            full.at[k, r, t], full.at[k, r, t], ag_s.at[k, r, s], ag_r.at[k, r, s], peer
        )

    def ag_step(k, r, s):
        ag_arrival(k, r, s).wait_recv()
        ag_copy(k, r, s + 1).start()

    own_copies[0].wait()
    own_copies[1].wait()
    weight_arrivals[0].wait_recv()
    weight_arrivals[1].wait_recv()
    loop(1, NQ, lambda k: rows_arrival(0, rem(q + k, NQ)).wait_recv())
    order_rows(0)
    for j in range(2):
        for r in range(2):
            cols = slice(r * HH, (r + 1) * HH)
            part[j, r, :, :, 0:HH] = (
                dot_nn(rows[0, j], wg[j, :, cols]).astype(BF).reshape(Z, S * CAP, HH)
            )
            part[j, r, :, :, HH:H] = (
                dot_nn(rows[0, j], wu[j, :, cols]).astype(BF).reshape(Z, S * CAP, HH)
            )
            rs_copy(j, r, 0).start()

    p1_reduce()

    own_copies[2].wait()
    weight_arrivals[2].wait_recv()
    loop(1, NQ, lambda k: rows_arrival(1, rem(q + k, NQ)).wait_recv())
    order_rows(1)
    for r in range(2):
        units = slice(r * HH, (r + 1) * HH)
        for j in range(2):
            value = dot_nt(rows[1, j, :, 0:W], wd[0, j, units, :]) + dot_nt(
                rows[1, j, :, W : 2 * W], wd[1, j, units, :]
            )
            part[2, r, :, :, j * HH : (j + 1) * HH] = value.astype(BF).reshape(Z, S * CAP, HH)
        rs_copy(2, r, 0).start()

    p1_finish()
    sums = sum_out[...].reshape(TOK, 2 * EL)
    weights_exp = jnp.exp(sums[:, 0:E])
    prob_ref[...] = weights_exp / jnp.sum(weights_exp, axis=1, keepdims=True)

    slot_row = lax.broadcasted_iota(jnp.int32, (NE, PAIR, 2 * EL), 1)
    slot_owner = lax.broadcasted_iota(jnp.int32, (NE, PAIR, 2 * EL), 0)
    slot_lane = lax.broadcasted_iota(jnp.int32, (NE, PAIR, 2 * EL), 2)
    slot_expert = slot_owner * 4 + c * 2 + jnp.where(slot_row >= CAP, 1, 0)
    holder = div(xy, S) == z
    spot = rem(xy, S)

    def w_copy(j):
        return remote(w_send.at[j], w_in.at[spot], wt_s.at[j], wt_r.at[spot], (dp, j))

    def w_arrival(b):
        return remote(w_send.at[b], w_in.at[b], wt_s.at[b], wt_r.at[b], (dp, z * S + b))

    @pl.when(holder)
    def _():
        spread = dot_nn(place[:, c].reshape(NE * PAIR, TOK), prob_ref[...].astype(BF))
        if E < 2 * EL:
            spread = jnp.concatenate(
                [spread, jnp.zeros((NE * PAIR, 2 * EL - E), F32)], axis=1
            )
        spread = jnp.where(slot_lane == slot_expert, spread.reshape(NE, PAIR, 2 * EL), 0.0)
        column = jnp.sum(spread, axis=2, keepdims=True)
        w_send[...] = jnp.broadcast_to(column, (NE, PAIR, 2 * EL)).astype(BF)
        loop(1, NE, lambda k: w_copy(rem(xy + k, NE)).start())
        w_in[spot] = w_send[xy]

    def rs_round(u):
        for k in range(3):
            lag = RS_LAG if k == 2 else 0

            def steps(k=k, lag=lag):
                for r in range(2):
                    rs_step(k, r, u - lag)

            if lag == 0:
                pl.when(u < Z - 2)(steps)
            else:
                pl.when(u >= lag)(steps)

    loop(0, Z - 2 + RS_LAG, rs_round)

    for b in range(S):

        @pl.when(z * S + b != xy)
        def _(b=b):
            w_arrival(b).wait_recv()

    for k in range(3):
        for r in range(2):
            rs_copy(k, r, Z - 2).wait_recv()
    dots = []
    for j in range(2):
        weight = jnp.concatenate(
            [w_in[b].astype(F32)[j * CAP : (j + 1) * CAP, 0:1] for b in range(S)], axis=0
        )
        dot = jnp.zeros((S * CAP, 1), F32)
        for r in range(2):
            both = part[j, r, z].astype(F32) + recv[j, r, Z - 2].astype(F32)
            cols = slice(j * HH, (j + 1) * HH)
            raw = part[2, r, z, :, cols].astype(F32) + recv[2, r, Z - 2, :, cols].astype(F32)
            gate = both[:, 0:HH]
            up = both[:, HH:H]
            sig = 1.0 / (1.0 + jnp.exp(-gate))
            silu = gate * sig
            hidden = silu * up
            d_hidden = raw * weight
            full[j, r, z, :, 0:HH] = (
                d_hidden * up * sig * (1.0 + gate * (1.0 - sig))
            ).astype(BF)
            full[j, r, z, :, HH:H] = (d_hidden * silu).astype(BF)
            full[2, r, z, :, cols] = (hidden * weight).astype(BF)
            dot = dot + jnp.sum(hidden * raw, axis=1, keepdims=True)
            ag_copy(j, r, 0).start()
        dots.append(dot)

    def dots_copy(b):
        return remote(
            dots_send.at[b], dots_in.at[xy], dt_s.at[b], dt_r.at[xy], (dp, z * S + b)
        )

    def dots_arrival(j):
        return remote(dots_send.at[0], dots_in.at[j], dt_s.at[0], dt_r.at[j], (dp, j))

    lane_two = lax.broadcasted_iota(jnp.int32, (PAIR, 2 * EL), 1)
    for b in range(S):
        value = jnp.concatenate(
            [dots[0][b * CAP : (b + 1) * CAP], dots[1][b * CAP : (b + 1) * CAP]], axis=0
        )
        value = jnp.broadcast_to(value, (PAIR, 2 * EL))
        high = value.astype(BF).astype(F32)
        dots_send[b] = jnp.where(lane_two < EL, high, value - high).astype(BF)

        @pl.when(z * S + b != xy)
        def _(b=b):
            dots_copy(b).start()

        @pl.when(z * S + b == xy)
        def _(b=b):
            dots_in[xy] = dots_send[b]

    def ag_round(u):
        for k in range(3):
            lag = AG_LAG if k == 2 else 0

            def steps(k=k, lag=lag):
                for r in range(2):
                    ag_step(k, r, u - lag)

            if lag == 0:
                pl.when(u < Z - 2)(steps)
            else:

                @pl.when(u == lag - 1)
                def _():
                    for r in range(2):
                        ag_copy(2, r, 0).start()

                pl.when(u >= lag)(steps)

    first_stop, second_stop = min(1, Z - 2), min(3, Z - 2)
    loop(0, first_stop, ag_round)

    def top_copy(j):
        return remote(top_send, top_in.at[c], tp_s.at[j], tp_r.at[c], (j, xy))

    def top_arrival(h):
        return remote(
            top_send, top_in.at[h], tp_s.at[h], tp_r.at[h], (div(xy, S) * CORES + h, xy)
        )

    @pl.when(holder)
    def _():
        loop(1, NE, lambda k: dots_arrival(rem(xy + k, NE)).wait_recv())
        lane_e = jnp.where(slot_lane >= EL, slot_lane - EL, slot_lane)
        masked = jnp.where(lane_e == slot_expert, dots_in[...].astype(F32), 0.0).astype(BF)
        top = dot_tn(
            place[:, c].reshape(NE * PAIR, TOK), masked.reshape(NE * PAIR, 2 * EL)
        )
        top_send[...] = top.astype(BF)
        loop(1, ND, lambda k: top_copy(rem(dp + k, ND)).start())
        top_in[c] = top_send[...]

    loop(first_stop, second_stop, ag_round)

    for h in range(CORES):

        @pl.when(div(xy, S) * CORES + h != dp)
        def _(h=h):
            top_arrival(h).wait_recv()

    top = top_in[0].astype(F32) + top_in[1].astype(F32)
    top = top[:, 0:E] + top[:, EL : EL + E]
    mean = sum_out[...].reshape(TOK, 2 * EL)[:, EL : EL + E]
    route = routing[...]
    chosen = jnp.zeros((TOK, E), F32)
    for k in range(route.shape[1]):
        chosen = chosen + jnp.where(route[:, k : k + 1] == lane, 1.0, 0.0)
    d_prob = jnp.where(chosen > 0.5, top, mean)
    prob = prob_ref[...]
    dlogits = prob * (d_prob - jnp.sum(prob * d_prob, axis=1, keepdims=True))
    high, low = split_two(dlogits)
    dlog_hi[...] = high
    dlog_lo[...] = low
    router_part = dot_tn(tokens[...], high) + dot_tn(tokens[...], low)
    gr_src[...] = packed(router_part[0:TOK], router_part[TOK : 2 * TOK], NE)
    p2_send()

    loop(second_stop, Z - 2, ag_round)
    p2_reduce()

    for k in range(2):
        for r in range(2):
            ag_arrival(k, r, Z - 2).wait_recv()

    for j in range(2):
        total = None
        for r in range(2):
            cols = slice(r * HH, (r + 1) * HH)
            both = full[j, r].reshape(ROWS, H)
            term = dot_nt(both[:, 0:HH], wg[j, :, cols]) + dot_nt(both[:, HH:H], wu[j, :, cols])
            total = term if total is None else total + term
        dx_ref[j] = total

    def back_copy(q2):
        return remote(
            back_send.at[div(q2, CORES), rem(q2, CORES)], back_in.at[q],
            bk_s.at[q2], bk_r.at[q], plane_peer(q2),
        )

    def back_arrival(q2):
        return remote(
            back_send.at[div(q2, CORES), rem(q2, CORES)], back_in.at[q2],
            bk_s.at[q2], bk_r.at[q2], plane_peer(q2),
        )

    def order_back(i):
        at = pl.ds(pl.multiple_of(i * CAP, CAP), CAP)
        block = jnp.concatenate([dx_ref[0, at, :], dx_ref[1, at, :]], axis=0).astype(BF)
        for h in range(CORES):
            back_send[i, h] = block[:, h * W : (h + 1) * W]

    loop(0, NE, order_back)
    loop(1, NQ, lambda k: back_copy(rem(q + k, NQ)).start())
    back_in[q] = back_send[xy, c]

    loop(Z - 2, Z - 2 + AG_LAG, ag_round)

    def out_copies(i, j):
        expert = c * 2 + j
        out = (grad_gate, grad_up, grad_down)[i]
        buf = (out_gate, out_up, out_down)[i]
        if i < 2:
            keep, give = buf.at[j, half, :], buf.at[j, other_half, :]
        else:
            keep, give = buf.at[c, j], buf.at[other, j]
        local = pltpu.make_async_copy(keep, out.at[expert], ol_s.at[i, j])
        send = remote(give, out.at[expert], ox_s.at[i, j], ox_r.at[i, j], twin)
        arrival = remote(give, out.at[other * 2 + j], ox_s.at[i, j], ox_r.at[i, j], twin)
        return local, send, arrival

    for j in range(2):
        for r in range(2):
            cols = slice(r * HH, (r + 1) * HH)
            both = full[j, r].reshape(ROWS, H)
            out_gate[j, :, cols] = dot_tn(rows[0, j], both[:, 0:HH]).astype(BF)
            out_up[j, :, cols] = dot_tn(rows[0, j], both[:, HH:H]).astype(BF)
        for i in range(2):
            local, send, _ = out_copies(i, j)
            send.start()
            local.start()

    for r in range(2):
        ag_arrival(2, r, Z - 2).wait_recv()
    for j in range(2):
        for r in range(2):
            units = slice(r * HH, (r + 1) * HH)
            hid = full[2, r, :, :, j * HH : (j + 1) * HH].reshape(ROWS, HH)
            value = dot_tn(hid, rows[1, j]).astype(BF)
            out_down[0, j, units, :] = value[:, 0:W]
            out_down[1, j, units, :] = value[:, W : 2 * W]
        local, send, _ = out_copies(2, j)
        send.start()
        local.start()

    p2_finish()
    packed_sum = gr_out[...].reshape(TOK, 2 * EL)
    grad_router[0:TOK, :] = packed_sum[:, 0:E]
    grad_router[TOK : 2 * TOK, :] = packed_sum[:, EL : EL + E]
    loop(1, NQ, lambda k: back_arrival(rem(q + k, NQ)).wait_recv())
    router_term = dot_nt(dlog_hi[...], w_router[...]) + dot_nt(dlog_lo[...], w_router[...])
    token_term = dot_tn(
        place[...].reshape(E * CAP, TOK), back_in[...].reshape(E * CAP, W)
    )
    grad_tokens[...] = (token_term + router_term).astype(BF)

    loop(1, NQ, lambda k: rows_copy(0, rem(q + k, NQ)).wait_send())
    loop(1, NQ, lambda k: rows_copy(1, rem(q + k, NQ)).wait_send())
    loop(1, NQ, lambda k: back_copy(rem(q + k, NQ)).wait_send())
    for copy in weight_copies:
        copy.wait_send()
    p1_drain()
    p2_drain()

    def ring_drain(s):
        for k in range(3):
            for r in range(2):
                rs_copy(k, r, s).wait_send()
                ag_copy(k, r, s).wait_send()

    loop(0, Z - 1, ring_drain)

    @pl.when(holder)
    def _():
        loop(1, NE, lambda k: w_copy(rem(xy + k, NE)).wait_send())
        loop(1, ND, lambda k: top_copy(rem(dp + k, ND)).wait_send())

    for b in range(S):

        @pl.when(z * S + b != xy)
        def _(b=b):
            dots_copy(b).wait_send()

    for i in range(3):
        for j in range(2):
            local, send, arrival = out_copies(i, j)
            local.wait()
            send.wait_send()
            arrival.wait_recv()


def per_device(tokens, cotangent, routing, w_router, running_mean, w_gate, w_up, w_down):
    NE = lax.axis_size("expert")
    ND = lax.axis_size("dp")
    Z = ND // CORES
    local_count, W, H = w_gate.shape
    E = NE * local_count
    TOK, top = routing.shape
    CAP = 3 * TOK * top // (2 * E)
    NQ = NE * CORES
    S = NE // Z
    PAIR, ROWS, HH = 2 * CAP, NE * CAP, H // 2
    sizes = (NE, Z, E, TOK, H, W, CAP)
    vmem = pl.BlockSpec(memory_space=pltpu.VMEM)
    hbm = pl.BlockSpec(memory_space=pl.ANY)
    dma = pltpu.SemaphoreType.DMA
    scratch = [
        pltpu.VMEM((NE, CORES, PAIR, TOK), BF),
        pltpu.VMEM((2, NQ, PAIR, W), BF),
        pltpu.VMEM((2, CORES, NE, PAIR, W), BF),
        pltpu.VMEM((2, 2, ROWS, 2 * W), BF),
        pltpu.VMEM((2, 2 * W, H), BF),
        pltpu.VMEM((2, 2 * W, H), BF),
        pltpu.VMEM((2, 2, H, W), BF),
        pltpu.VMEM((3, 2, Z, S * CAP, H), BF),
        pltpu.VMEM((3, 2, Z - 1, S * CAP, H), BF),
        pltpu.VMEM((3, 2, Z, S * CAP, H), BF),
        pltpu.VMEM((ND, TOK // ND, 128), F32),
        pltpu.VMEM((ND, TOK // ND, 128), F32),
        pltpu.VMEM((ND, TOK // ND, 128), F32),
        pltpu.VMEM((NE, TOK // NE, 128), F32),
        pltpu.VMEM((NE, TOK // NE, 128), F32),
        pltpu.VMEM((NE, TOK // NE, 128), F32),
        pltpu.VMEM((TOK, E), F32),
        pltpu.VMEM((NE, PAIR, 128), BF),
        pltpu.VMEM((S, PAIR, 128), BF),
        pltpu.VMEM((S, PAIR, 128), BF),
        pltpu.VMEM((NE, PAIR, 128), BF),
        pltpu.VMEM((TOK, 128), BF),
        pltpu.VMEM((2, TOK, 128), BF),
        pltpu.VMEM((TOK, E), BF),
        pltpu.VMEM((TOK, E), BF),
        pltpu.VMEM((2, ROWS, 2 * W), F32),
        pltpu.VMEM((NE, CORES, PAIR, W), BF),
        pltpu.VMEM((NQ, PAIR, W), BF),
        pltpu.VMEM((2, 2 * W, H), BF),
        pltpu.VMEM((2, 2 * W, H), BF),
        pltpu.VMEM((2, 2, H, W), BF),
        dma((2, NQ)), dma((2, NQ)),
        dma((3,)), dma((3,)), dma((3,)),
        dma((2, ND)), dma((2, ND)),
        dma((2, NE)), dma((2, NE)),
        dma((3, 2, Z - 1)), dma((3, 2, Z - 1)),
        dma((3, 2, Z - 1)), dma((3, 2, Z - 1)),
        dma((NE,)), dma((S,)),
        dma((S,)), dma((NE,)),
        dma((ND,)), dma((2,)),
        dma((NQ,)), dma((NQ,)),
        dma((3, 2)), dma((3, 2)), dma((3, 2)),
    ]
    return pl.pallas_call(
        functools.partial(kernel, sizes),
        out_shape=(
            jax.ShapeDtypeStruct((TOK, W), BF),
            jax.ShapeDtypeStruct((W, E), F32),
            jax.ShapeDtypeStruct((local_count, W, H), BF),
            jax.ShapeDtypeStruct((local_count, W, H), BF),
            jax.ShapeDtypeStruct((local_count, H, W), BF),
        ),
        in_specs=[vmem] * 5 + [hbm] * 3,
        out_specs=(vmem, vmem, hbm, hbm, hbm),
        scratch_shapes=scratch,
        compiler_params=pltpu.CompilerParams(
            collective_id=0, has_side_effects=True, vmem_limit_bytes=56 * 1024 * 1024
        ),
        cost_estimate=pl.CostEstimate(
            flops=6 * 10**9, bytes_accessed=10**7, transcendentals=10**5
        ),
    )(tokens, cotangent, routing, w_router, running_mean, w_gate, w_up, w_down)


def solution(mesh):
    return jax.shard_map(
        per_device,
        mesh=mesh,
        in_specs=(
            P("expert", "dp"),
            P("expert", "dp"),
            P("expert", None),
            P("dp", None),
            P(None, "dp"),
            P("expert", "dp", None),
            P("expert", "dp", None),
            P("expert", None, "dp"),
        ),
        out_specs=(
            P("expert", "dp"),
            P("dp", None),
            P("expert", "dp", None),
            P("expert", "dp", None),
            P("expert", None, "dp"),
        ),
        check_vma=False,
    )
```

```python
import functools

import jax
import jax.numpy as jnp
from jax import lax
from jax.experimental import pallas as pl
from jax.experimental.pallas import tpu as pltpu
from jax.sharding import PartitionSpec as P

MESH = pl.DeviceIdType.MESH
BF = jnp.bfloat16
F32 = jnp.float32
CORES = 2
RS_LAG = 3
AG_LAG = 3


def rem(a, n):
    return lax.rem(a, jnp.int32(n))


def div(a, n):
    return lax.div(a, jnp.int32(n))


def remote(src, dst, send_sem, recv_sem, device):
    return pltpu.make_async_remote_copy(
        src_ref=src,
        dst_ref=dst,
        send_sem=send_sem,
        recv_sem=recv_sem,
        device_id=device,
        device_id_type=MESH,
    )


def loop(lower, upper, body):
    def step(i, carry):
        body(i)
        return carry

    lax.fori_loop(lower, upper, step, 0)


def dot_nn(a, b):
    return jnp.dot(a, b, preferred_element_type=F32)


def dot_nt(a, b):
    return lax.dot_general(a, b, (((1,), (1,)), ((), ())), preferred_element_type=F32)


def dot_tn(a, b):
    return lax.dot_general(a, b, (((0,), (0,)), ((), ())), preferred_element_type=F32)


def split_two(value):
    high = value.astype(BF)
    low = (value - high.astype(F32)).astype(BF)
    return high, low


def kernel(
    sizes,
    tokens, cotangent, routing, w_router, running_mean, w_gate, w_up, w_down,
    grad_tokens, grad_router, grad_gate, grad_up, grad_down,
    place, send_rows, in_rows, rows, wg, wu, wd,
    part, recv, full,
    sum_src, sum_in, sum_out, gr_src, gr_in, gr_out,
    prob_ref, chosen_ref, w_send, w_in, dots_send, dots_in, top_send, top_in, dlog_hi, dlog_lo,
    dx_ref, back_send, back_in, out_gate, out_up, out_down,
    rows_s, rows_r, wx_s, wx_r, wl_s,
    p1_s, p1_r, p2_s, p2_r,
    rs_s, rs_r, ag_s, ag_r,
    wt_s, wt_r, dt_s, dt_r, tp_s, tp_r, bk_s, bk_r,
    ol_s, ox_s, ox_r,
):
    NE, Z, E, TOK, H, W, CAP = sizes
    ND = Z * CORES
    NQ = NE * CORES
    S = NE // Z
    HH = H // 2
    EL = 64
    GB = NE // (W // 128)
    PAIR = 2 * CAP
    ROWS = NE * CAP

    dp = lax.axis_index("dp")
    xy = lax.axis_index("expert")
    z = div(dp, CORES)
    c = rem(dp, CORES)
    other = 1 - c
    q = xy * CORES + c
    right = rem(z + 1, Z)
    left = rem(z + Z - 1, Z)
    twin = (z * CORES + other, xy)

    def plane_peer(q2):
        return (z * CORES + rem(q2, CORES), div(q2, CORES))

    side = 4 if NE % 4 == 0 else NE

    def ahead(k):
        a, rest = rem(k, side), div(k, side)
        b, d = rem(rest, NE // side), div(rest, NE // side)
        x2 = rem(rem(xy, side) + a, side)
        y2 = rem(div(xy, side) + b, NE // side)
        return (y2 * side + x2) * CORES + rem(c + d, CORES)

    def behind(k):
        a, rest = rem(k, side), div(k, side)
        b, d = rem(rest, NE // side), div(rest, NE // side)
        x2 = rem(rem(xy, side) + side - a, side)
        y2 = rem(div(xy, side) + NE // side - b, NE // side)
        return (y2 * side + x2) * CORES + rem(c + CORES - d, CORES)

    barrier = pltpu.get_barrier_semaphore()

    def greet_plane(k):
        pl.semaphore_signal(
            barrier, inc=1, device_id=plane_peer(rem(q + k, NQ)), device_id_type=MESH
        )

    def greet_column(m):
        z2 = rem(z + 1 + div(m, CORES), Z)
        pl.semaphore_signal(
            barrier, inc=1, device_id=(z2 * CORES + rem(m, CORES), xy), device_id_type=MESH
        )

    loop(1, NQ, greet_plane)
    loop(0, CORES * (Z - 1), greet_column)

    def own_weights(i, src, dst):
        return pltpu.make_async_copy(src, dst, wl_s.at[i])

    half = pl.ds(pl.multiple_of(c * W, W), W)
    mine = pl.ds(c * 2, 2)
    theirs = pl.ds(other * 2, 2)
    own_copies = [
        own_weights(0, w_gate.at[mine], wg.at[:, half, :]),
        own_weights(1, w_up.at[mine], wu.at[:, half, :]),
        own_weights(2, w_down.at[mine], wd.at[c]),
    ]
    for copy in own_copies:
        copy.start()

    route = routing[...]
    row_e = lax.broadcasted_iota(jnp.int32, (E, TOK), 0)
    has = jnp.zeros((E, TOK), F32)
    for k in range(route.shape[0]):
        has = has + jnp.where(route[k : k + 1, :] == row_e, 1.0, 0.0)
    t_row = lax.broadcasted_iota(jnp.int32, (TOK, TOK), 0)
    t_col = lax.broadcasted_iota(jnp.int32, (TOK, TOK), 1)
    before = jnp.where(t_row < t_col, 1.0, 0.0).astype(BF)
    same = jnp.where(t_row == t_col, 1.0, 0.0).astype(BF)
    pos = jnp.where(has > 0.5, dot_nn(has.astype(BF), before), -1.0)
    chosen_ref[...] = dot_nt(same, has.astype(BF))
    slot_iota = lax.broadcasted_iota(jnp.int32, (E, CAP, TOK), 1).astype(F32)
    placing = jnp.where(pos[:, None, :] == slot_iota, 1.0, 0.0)
    placing = placing.reshape(E * CAP, TOK).astype(BF)
    place[...] = placing.reshape(NE, CORES, PAIR, TOK)
    send_rows[0] = dot_nn(placing, tokens[...]).astype(BF).reshape(NQ, PAIR, W)
    send_rows[1] = dot_nn(placing, cotangent[...]).astype(BF).reshape(NQ, PAIR, W)

    pl.semaphore_wait(barrier, NQ - 1 + CORES * (Z - 1))

    def rows_copy(which, q2):
        return remote(
            send_rows.at[which, q2], in_rows.at[which, c, xy],
            rows_s.at[which, q2], rows_r.at[which, q], plane_peer(q2),
        )

    def rows_arrival(which, q2):
        return remote(
            send_rows.at[which, q2], in_rows.at[which, rem(q2, CORES), div(q2, CORES)],
            rows_s.at[which, q2], rows_r.at[which, q2], plane_peer(q2),
        )

    weight_copies = [
        remote(w_gate.at[theirs], wg.at[:, half, :], wx_s.at[0], wx_r.at[0], twin),
        remote(w_up.at[theirs], wu.at[:, half, :], wx_s.at[1], wx_r.at[1], twin),
        remote(w_down.at[theirs], wd.at[c], wx_s.at[2], wx_r.at[2], twin),
    ]
    other_half = pl.ds(pl.multiple_of(other * W, W), W)
    weight_arrivals = [
        remote(w_gate.at[theirs], wg.at[:, other_half, :], wx_s.at[0], wx_r.at[0], twin),
        remote(w_up.at[theirs], wu.at[:, other_half, :], wx_s.at[1], wx_r.at[1], twin),
        remote(w_down.at[theirs], wd.at[other], wx_s.at[2], wx_r.at[2], twin),
    ]
    weight_copies[0].start()
    weight_copies[1].start()
    loop(1, NQ, lambda k: rows_copy(0, ahead(k)).start())
    in_rows[0, c, xy] = send_rows[0, q]
    in_rows[1, c, xy] = send_rows[1, q]

    def sum_blocks(n, index, peer, src, into, out, sem_s, sem_r):
        def scatter(j):
            return remote(src.at[j], into.at[index], sem_s.at[0, j], sem_r.at[0, index], peer(j))

        def scatter_arrival(j):
            return remote(src.at[j], into.at[j], sem_s.at[0, j], sem_r.at[0, j], peer(j))

        def gather(j):
            return remote(
                out.at[index], out.at[index], sem_s.at[1, j], sem_r.at[1, index], peer(j)
            )

        def gather_arrival(j):
            return remote(out.at[j], out.at[j], sem_s.at[1, j], sem_r.at[1, j], peer(j))

        def send():
            loop(1, n, lambda k: scatter(rem(index + k, n)).start())
            into[index] = src[index]

        def reduce():
            loop(1, n, lambda k: scatter_arrival(rem(index + k, n)).wait_recv())
            out[index] = jnp.sum(into[...], axis=0)
            loop(1, n, lambda k: gather(rem(index + k, n)).start())

        def finish():
            loop(1, n, lambda k: gather_arrival(rem(index + k, n)).wait_recv())

        def drain():
            loop(1, n, lambda k: scatter(rem(index + k, n)).wait_send())
            loop(1, n, lambda k: gather(rem(index + k, n)).wait_send())

        return send, reduce, finish, drain

    p1_send, p1_reduce, p1_finish, p1_drain = sum_blocks(
        ND, dp, lambda j: (j, xy), sum_src, sum_in, sum_out, p1_s, p1_r
    )
    p2_send, p2_reduce, p2_finish, p2_drain = sum_blocks(
        NE, xy, lambda j: (dp, j), gr_src, gr_in, gr_out, p2_s, p2_r
    )

    def packed(first, second, count):
        if E < EL:
            gap = jnp.zeros((TOK, EL - E), F32)
            first = jnp.concatenate([first, gap], axis=1)
            second = jnp.concatenate([second, gap], axis=1)
        return jnp.concatenate([first, second], axis=1).reshape(count, TOK // count, 2 * EL)

    logits_part = dot_nt(tokens[...], w_router[...])
    mean_part = dot_nt(cotangent[...], running_mean[...])
    sum_src[...] = packed(logits_part, mean_part, ND)
    p1_send()

    def order_rows(which):
        def body(p):
            for h in range(CORES):
                block = in_rows[which, h, pl.ds(p * 2, 2)].astype(F32)
                for j in range(2):
                    piece = block[:, j * CAP : (j + 1) * CAP, :].reshape(PAIR, W)
                    rows[
                        which, j, pl.ds(pl.multiple_of(p * PAIR, PAIR), PAIR), h * W : (h + 1) * W
                    ] = piece.astype(BF)

        loop(0, NE // 2, body)

    def rs_copy(k, r, s):
        t = rem(z - 1 - s + 2 * Z, Z) if r == 0 else rem(z + 1 + s, Z)
        peer = ((right if r == 0 else left) * CORES + c, xy)
        return remote(
            part.at[k, r, t], recv.at[k, r, s], rs_s.at[k, r, s], rs_r.at[k, r, s], peer
        )

    def rs_step(k, r, s):
        rs_copy(k, r, s).wait_recv()
        t = rem(z - 2 - s + 2 * Z, Z) if r == 0 else rem(z + 2 + s, Z)
        part[k, r, t] = (part[k, r, t].astype(F32) + recv[k, r, s].astype(F32)).astype(BF)
        rs_copy(k, r, s + 1).start()

    def ag_copy(k, r, s):
        t = rem(z - s + Z, Z) if r == 0 else rem(z + s, Z)
        peer = ((right if r == 0 else left) * CORES + c, xy)
        return remote(
            full.at[k, r, t], full.at[k, r, t], ag_s.at[k, r, s], ag_r.at[k, r, s], peer
        )

    def ag_arrival(k, r, s):
        t = rem(z - 1 - s + Z, Z) if r == 0 else rem(z + 1 + s, Z)
        peer = ((right if r == 0 else left) * CORES + c, xy)
        return remote(
            full.at[k, r, t], full.at[k, r, t], ag_s.at[k, r, s], ag_r.at[k, r, s], peer
        )

    def ag_step(k, r, s):
        ag_arrival(k, r, s).wait_recv()
        ag_copy(k, r, s + 1).start()

    own_copies[0].wait()
    own_copies[1].wait()
    weight_arrivals[0].wait_recv()
    weight_arrivals[1].wait_recv()
    def rows_then_grads(k):
        rows_arrival(0, behind(k)).wait_recv()
        rows_copy(1, ahead(k)).start()

    loop(1, NQ, rows_then_grads)
    weight_copies[2].start()
    order_rows(0)
    for j in range(2):
        for r in range(2):
            cols = slice(r * HH, (r + 1) * HH)
            part[j, r, :, :, 0:HH] = (
                dot_nn(rows[0, j], wg[j, :, cols]).astype(BF).reshape(Z, S * CAP, HH)
            )
            part[j, r, :, :, HH:H] = (
                dot_nn(rows[0, j], wu[j, :, cols]).astype(BF).reshape(Z, S * CAP, HH)
            )
            rs_copy(j, r, 0).start()

    p1_reduce()

    def rs_round(u):
        for k in range(3):
            lag = RS_LAG if k == 2 else 0

            def steps(k=k, lag=lag):
                for r in range(2):
                    rs_step(k, r, u - lag)

            if lag == 0:
                pl.when(u < Z - 2)(steps)
            else:
                pl.when(u >= lag)(steps)

    loop(0, RS_LAG, rs_round)

    own_copies[2].wait()
    weight_arrivals[2].wait_recv()
    loop(1, NQ, lambda k: rows_arrival(1, rem(q + k, NQ)).wait_recv())
    order_rows(1)
    for r in range(2):
        units = slice(r * HH, (r + 1) * HH)
        for j in range(2):
            value = dot_nt(rows[1, j, :, 0:W], wd[0, j, units, :]) + dot_nt(
                rows[1, j, :, W : 2 * W], wd[1, j, units, :]
            )
            part[2, r, :, :, j * HH : (j + 1) * HH] = value.astype(BF).reshape(Z, S * CAP, HH)
        rs_copy(2, r, 0).start()

    p1_finish()
    sums = sum_out[...].reshape(TOK, 2 * EL)
    weights_exp = jnp.exp(sums[:, 0:E])
    prob_ref[...] = weights_exp / jnp.sum(weights_exp, axis=1, keepdims=True)

    slot_row = lax.broadcasted_iota(jnp.int32, (NE, PAIR, 2 * EL), 1)
    slot_owner = lax.broadcasted_iota(jnp.int32, (NE, PAIR, 2 * EL), 0)
    slot_lane = lax.broadcasted_iota(jnp.int32, (NE, PAIR, 2 * EL), 2)
    slot_expert = slot_owner * 4 + c * 2 + jnp.where(slot_row >= CAP, 1, 0)
    holder = div(xy, S) == z
    spot = rem(xy, S)

    def w_copy(j):
        return remote(w_send.at[j], w_in.at[spot], wt_s.at[j], wt_r.at[spot], (dp, j))

    def w_arrival(b):
        return remote(w_send.at[b], w_in.at[b], wt_s.at[b], wt_r.at[b], (dp, z * S + b))

    @pl.when(holder)
    def _():
        spread = dot_nn(place[:, c].reshape(NE * PAIR, TOK), prob_ref[...].astype(BF))
        if E < 2 * EL:
            spread = jnp.concatenate(
                [spread, jnp.zeros((NE * PAIR, 2 * EL - E), F32)], axis=1
            )
        spread = jnp.where(slot_lane == slot_expert, spread.reshape(NE, PAIR, 2 * EL), 0.0)
        column = jnp.sum(spread, axis=2, keepdims=True)
        w_send[...] = jnp.broadcast_to(column, (NE, PAIR, 2 * EL)).astype(BF)
        loop(1, NE, lambda k: w_copy(rem(xy + k, NE)).start())
        w_in[spot] = w_send[xy]

    loop(RS_LAG, Z - 2 + RS_LAG, rs_round)

    for b in range(S):

        @pl.when(z * S + b != xy)
        def _(b=b):
            w_arrival(b).wait_recv()

    for k in range(3):
        for r in range(2):
            rs_copy(k, r, Z - 2).wait_recv()
    dots = []
    for j in range(2):
        weight = jnp.concatenate(
            [w_in[b].astype(F32)[j * CAP : (j + 1) * CAP, 0:1] for b in range(S)], axis=0
        )
        dot = jnp.zeros((S * CAP, 1), F32)
        for r in range(2):
            both = part[j, r, z].astype(F32) + recv[j, r, Z - 2].astype(F32)
            cols = slice(j * HH, (j + 1) * HH)
            raw = part[2, r, z, :, cols].astype(F32) + recv[2, r, Z - 2, :, cols].astype(F32)
            gate = both[:, 0:HH]
            up = both[:, HH:H]
            sig = 1.0 / (1.0 + jnp.exp(-gate))
            silu = gate * sig
            hidden = silu * up
            d_hidden = raw * weight
            full[j, r, z, :, 0:HH] = (
                d_hidden * up * sig * (1.0 + gate * (1.0 - sig))
            ).astype(BF)
            full[j, r, z, :, HH:H] = (d_hidden * silu).astype(BF)
            full[2, r, z, :, cols] = (hidden * weight).astype(BF)
            dot = dot + jnp.sum(hidden * raw, axis=1, keepdims=True)
            ag_copy(j, r, 0).start()
        dots.append(dot)

    def dots_copy(b):
        return remote(
            dots_send.at[b], dots_in.at[xy], dt_s.at[b], dt_r.at[xy], (dp, z * S + b)
        )

    def dots_arrival(j):
        return remote(dots_send.at[0], dots_in.at[j], dt_s.at[0], dt_r.at[j], (dp, j))

    lane_two = lax.broadcasted_iota(jnp.int32, (PAIR, 2 * EL), 1)
    for b in range(S):
        value = jnp.concatenate(
            [dots[0][b * CAP : (b + 1) * CAP], dots[1][b * CAP : (b + 1) * CAP]], axis=0
        )
        value = jnp.broadcast_to(value, (PAIR, 2 * EL))
        high = value.astype(BF).astype(F32)
        dots_send[b] = jnp.where(lane_two < EL, high, value - high).astype(BF)

        @pl.when(z * S + b != xy)
        def _(b=b):
            dots_copy(b).start()

        @pl.when(z * S + b == xy)
        def _(b=b):
            dots_in[xy] = dots_send[b]

    def ag_round(u):
        for k in range(3):
            lag = AG_LAG if k == 2 else 0

            def steps(k=k, lag=lag):
                for r in range(2):
                    ag_step(k, r, u - lag)

            if lag == 0:
                pl.when(u < Z - 2)(steps)
            else:

                @pl.when(u == lag - 1)
                def _():
                    for r in range(2):
                        ag_copy(2, r, 0).start()

                pl.when(u >= lag)(steps)

    loop(0, Z - 2, ag_round)

    for k in range(2):
        for r in range(2):
            ag_arrival(k, r, Z - 2).wait_recv()

    for j in range(2):
        total = None
        for r in range(2):
            cols = slice(r * HH, (r + 1) * HH)
            both = full[j, r].reshape(ROWS, H)
            term = dot_nt(both[:, 0:HH], wg[j, :, cols]) + dot_nt(both[:, HH:H], wu[j, :, cols])
            total = term if total is None else total + term
        dx_ref[j] = total

    def back_copy(q2):
        return remote(
            back_send.at[div(q2, CORES), rem(q2, CORES)], back_in.at[q],
            bk_s.at[q2], bk_r.at[q], plane_peer(q2),
        )

    def back_arrival(q2):
        return remote(
            back_send.at[div(q2, CORES), rem(q2, CORES)], back_in.at[q2],
            bk_s.at[q2], bk_r.at[q2], plane_peer(q2),
        )

    def order_back(i):
        at = pl.ds(pl.multiple_of(i * CAP, CAP), CAP)
        block = jnp.concatenate([dx_ref[0, at, :], dx_ref[1, at, :]], axis=0).astype(BF)
        for h in range(CORES):
            back_send[i, h] = block[:, h * W : (h + 1) * W]

    loop(0, NE, order_back)
    loop(1, NQ, lambda k: back_copy(ahead(k)).start())
    back_in[q] = back_send[xy, c]

    def top_copy(j):
        return remote(top_send, top_in.at[c], tp_s.at[j], tp_r.at[c], (j, xy))

    def top_arrival(h):
        return remote(
            top_send, top_in.at[h], tp_s.at[h], tp_r.at[h], (div(xy, S) * CORES + h, xy)
        )

    @pl.when(holder)
    def _():
        loop(1, NE, lambda k: dots_arrival(rem(xy + k, NE)).wait_recv())
        lane_e = jnp.where(slot_lane >= EL, slot_lane - EL, slot_lane)
        masked = jnp.where(lane_e == slot_expert, dots_in[...].astype(F32), 0.0).astype(BF)
        top = dot_tn(
            place[:, c].reshape(NE * PAIR, TOK), masked.reshape(NE * PAIR, 2 * EL)
        )
        top_send[...] = top.astype(BF)
        loop(1, ND, lambda k: top_copy(rem(dp + k, ND)).start())
        top_in[c] = top_send[...]

    loop(Z - 2, Z - 2 + AG_LAG, ag_round)

    def out_copies(i, j):
        expert = c * 2 + j
        out = (grad_gate, grad_up, grad_down)[i]
        buf = (out_gate, out_up, out_down)[i]
        if i < 2:
            keep, give = buf.at[j, half, :], buf.at[j, other_half, :]
        else:
            keep, give = buf.at[c, j], buf.at[other, j]
        local = pltpu.make_async_copy(keep, out.at[expert], ol_s.at[i, j])
        send = remote(give, out.at[expert], ox_s.at[i, j], ox_r.at[i, j], twin)
        arrival = remote(give, out.at[other * 2 + j], ox_s.at[i, j], ox_r.at[i, j], twin)
        return local, send, arrival

    for j in range(2):
        for r in range(2):
            cols = slice(r * HH, (r + 1) * HH)
            both = full[j, r].reshape(ROWS, H)
            out_gate[j, :, cols] = dot_tn(rows[0, j], both[:, 0:HH]).astype(BF)
            out_up[j, :, cols] = dot_tn(rows[0, j], both[:, HH:H]).astype(BF)
        for i in range(2):
            local, send, _ = out_copies(i, j)
            send.start()
            local.start()

    for h in range(CORES):

        @pl.when(div(xy, S) * CORES + h != dp)
        def _(h=h):
            top_arrival(h).wait_recv()

    top = top_in[0].astype(F32) + top_in[1].astype(F32)
    top = top[:, 0:E] + top[:, EL : EL + E]
    mean = sum_out[...].reshape(TOK, 2 * EL)[:, EL : EL + E]
    d_prob = jnp.where(chosen_ref[...] > 0.5, top, mean)
    prob = prob_ref[...]
    dlogits = prob * (d_prob - jnp.sum(prob * d_prob, axis=1, keepdims=True))
    high, low = split_two(dlogits)
    dlog_hi[...] = high
    dlog_lo[...] = low
    router_part = dot_tn(high, tokens[...]) + dot_tn(low, tokens[...])
    for h in range(W // 128):
        gr_src[h * GB : (h + 1) * GB] = router_part[:, h * 128 : (h + 1) * 128].reshape(
            GB, E // GB, 128
        )
    p2_send()

    for r in range(2):
        ag_arrival(2, r, Z - 2).wait_recv()
    for j in range(2):
        for r in range(2):
            units = slice(r * HH, (r + 1) * HH)
            hid = full[2, r, :, :, j * HH : (j + 1) * HH].reshape(ROWS, HH)
            value = dot_tn(hid, rows[1, j]).astype(BF)
            out_down[0, j, units, :] = value[:, 0:W]
            out_down[1, j, units, :] = value[:, W : 2 * W]
        local, send, _ = out_copies(2, j)
        send.start()
        local.start()

    p2_reduce()
    loop(1, NQ, lambda k: back_arrival(rem(q + k, NQ)).wait_recv())
    router_term = dot_nn(dlog_hi[...], w_router[...]) + dot_nn(dlog_lo[...], w_router[...])
    token_term = dot_tn(
        place[...].reshape(E * CAP, TOK), back_in[...].reshape(E * CAP, W)
    )
    grad_tokens[...] = (token_term + router_term).astype(BF)
    p2_finish()
    for h in range(W // 128):
        grad_router[:, h * 128 : (h + 1) * 128] = gr_out[h * GB : (h + 1) * GB].reshape(E, 128)

    loop(1, NQ, lambda k: rows_copy(0, rem(q + k, NQ)).wait_send())
    loop(1, NQ, lambda k: rows_copy(1, rem(q + k, NQ)).wait_send())
    loop(1, NQ, lambda k: back_copy(rem(q + k, NQ)).wait_send())
    for copy in weight_copies:
        copy.wait_send()
    p1_drain()
    p2_drain()

    def ring_drain(s):
        for k in range(3):
            for r in range(2):
                rs_copy(k, r, s).wait_send()
                ag_copy(k, r, s).wait_send()

    loop(0, Z - 1, ring_drain)

    @pl.when(holder)
    def _():
        loop(1, NE, lambda k: w_copy(rem(xy + k, NE)).wait_send())
        loop(1, ND, lambda k: top_copy(rem(dp + k, ND)).wait_send())

    for b in range(S):

        @pl.when(z * S + b != xy)
        def _(b=b):
            dots_copy(b).wait_send()

    for i in range(3):
        for j in range(2):
            local, send, arrival = out_copies(i, j)
            local.wait()
            send.wait_send()
            arrival.wait_recv()


def write_out(*refs):
    sources, targets, sems = refs[:5], refs[5:10], refs[10]
    copies = [
        pltpu.make_async_copy(sources[i], targets[i], sems.at[i]) for i in (2, 3, 4, 0, 1)
    ]
    for copy in copies:
        copy.start()
    for copy in copies:
        copy.wait()


def per_device(tokens, cotangent, routing, w_router, running_mean, w_gate, w_up, w_down):
    NE = lax.axis_size("expert")
    ND = lax.axis_size("dp")
    Z = ND // CORES
    local_count, W, H = w_gate.shape
    E = NE * local_count
    TOK, top = routing.shape
    routing, w_router = routing.T, w_router.T
    CAP = 3 * TOK * top // (2 * E)
    NQ = NE * CORES
    S = NE // Z
    PAIR, ROWS, HH = 2 * CAP, NE * CAP, H // 2
    sizes = (NE, Z, E, TOK, H, W, CAP)
    vmem = pl.BlockSpec(memory_space=pltpu.VMEM)
    hbm = pl.BlockSpec(memory_space=pl.ANY)
    dma = pltpu.SemaphoreType.DMA
    scratch = [
        pltpu.VMEM((NE, CORES, PAIR, TOK), BF),
        pltpu.VMEM((2, NQ, PAIR, W), BF),
        pltpu.VMEM((2, CORES, NE, PAIR, W), BF),
        pltpu.VMEM((2, 2, ROWS, 2 * W), BF),
        pltpu.VMEM((2, 2 * W, H), BF),
        pltpu.VMEM((2, 2 * W, H), BF),
        pltpu.VMEM((2, 2, H, W), BF),
        pltpu.VMEM((3, 2, Z, S * CAP, H), BF),
        pltpu.VMEM((3, 2, Z - 1, S * CAP, H), BF),
        pltpu.VMEM((3, 2, Z, S * CAP, H), BF),
        pltpu.VMEM((ND, TOK // ND, 128), F32),
        pltpu.VMEM((ND, TOK // ND, 128), F32),
        pltpu.VMEM((ND, TOK // ND, 128), F32),
        pltpu.VMEM((NE, E * W // (128 * NE), 128), F32),
        pltpu.VMEM((NE, E * W // (128 * NE), 128), F32),
        pltpu.VMEM((NE, E * W // (128 * NE), 128), F32),
        pltpu.VMEM((TOK, E), F32),
        pltpu.VMEM((TOK, E), F32),
        pltpu.VMEM((NE, PAIR, 128), BF),
        pltpu.VMEM((S, PAIR, 128), BF),
        pltpu.VMEM((S, PAIR, 128), BF),
        pltpu.VMEM((NE, PAIR, 128), BF),
        pltpu.VMEM((TOK, 128), BF),
        pltpu.VMEM((2, TOK, 128), BF),
        pltpu.VMEM((TOK, E), BF),
        pltpu.VMEM((TOK, E), BF),
        pltpu.VMEM((2, ROWS, 2 * W), F32),
        pltpu.VMEM((NE, CORES, PAIR, W), BF),
        pltpu.VMEM((NQ, PAIR, W), BF),
        pltpu.VMEM((2, 2 * W, H), BF),
        pltpu.VMEM((2, 2 * W, H), BF),
        pltpu.VMEM((2, 2, H, W), BF),
        dma((2, NQ)), dma((2, NQ)),
        dma((3,)), dma((3,)), dma((3,)),
        dma((2, ND)), dma((2, ND)),
        dma((2, NE)), dma((2, NE)),
        dma((3, 2, Z - 1)), dma((3, 2, Z - 1)),
        dma((3, 2, Z - 1)), dma((3, 2, Z - 1)),
        dma((NE,)), dma((S,)),
        dma((S,)), dma((NE,)),
        dma((ND,)), dma((2,)),
        dma((NQ,)), dma((NQ,)),
        dma((3, 2)), dma((3, 2)), dma((3, 2)),
    ]
    results = pl.pallas_call(
        functools.partial(kernel, sizes),
        out_shape=(
            pltpu.VMEM((TOK, W), BF),
            pltpu.VMEM((E, W), F32),
            pltpu.VMEM((local_count, W, H), BF),
            pltpu.VMEM((local_count, W, H), BF),
            pltpu.VMEM((local_count, H, W), BF),
        ),
        in_specs=[vmem] * 5 + [hbm] * 3,
        out_specs=(vmem, vmem, vmem, vmem, vmem),
        scratch_shapes=scratch,
        compiler_params=pltpu.CompilerParams(
            collective_id=0, has_side_effects=True, vmem_limit_bytes=56 * 1024 * 1024
        ),
        cost_estimate=pl.CostEstimate(
            flops=6 * 10**9, bytes_accessed=10**7, transcendentals=10**5
        ),
    )(tokens, cotangent, routing, w_router, running_mean, w_gate, w_up, w_down)
    grad_tokens, grad_router, *rest = pl.pallas_call(
        write_out,
        out_shape=[jax.ShapeDtypeStruct(x.shape, x.dtype) for x in results],
        in_specs=[hbm] * 5,
        out_specs=[hbm] * 5,
        scratch_shapes=[dma((5,))],
    )(*results)
    return (grad_tokens, grad_router.T, *rest)


def solution(mesh):
    return jax.shard_map(
        per_device,
        mesh=mesh,
        in_specs=(
            P("expert", "dp"),
            P("expert", "dp"),
            P("expert", None),
            P("dp", None),
            P(None, "dp"),
            P("expert", "dp", None),
            P("expert", "dp", None),
            P("expert", None, "dp"),
        ),
        out_specs=(
            P("expert", "dp"),
            P("dp", None),
            P("expert", "dp", None),
            P("expert", "dp", None),
            P("expert", None, "dp"),
        ),
        check_vma=False,
    )
```

```python
import functools

import jax
import jax.numpy as jnp
from jax import lax
from jax.experimental import pallas as pl
from jax.experimental.pallas import tpu as pltpu
from jax.sharding import PartitionSpec as P

MESH = pl.DeviceIdType.MESH
BF = jnp.bfloat16
F32 = jnp.float32
CORES = 2
ROWS_FIRST = 3
GRADS_FIRST = 0
GRADS_NEXT = 4


def rem(a, n):
    return lax.rem(a, jnp.int32(n))


def div(a, n):
    return lax.div(a, jnp.int32(n))


def remote(src, dst, send_sem, recv_sem, device):
    return pltpu.make_async_remote_copy(
        src_ref=src,
        dst_ref=dst,
        send_sem=send_sem,
        recv_sem=recv_sem,
        device_id=device,
        device_id_type=MESH,
    )


def loop(lower, upper, body):
    def step(i, carry):
        body(i)
        return carry

    lax.fori_loop(lower, upper, step, 0)


def dot_nn(a, b):
    return jnp.dot(a, b, preferred_element_type=F32)


def dot_nt(a, b):
    return lax.dot_general(a, b, (((1,), (1,)), ((), ())), preferred_element_type=F32)


def dot_tn(a, b):
    return lax.dot_general(a, b, (((0,), (0,)), ((), ())), preferred_element_type=F32)


def split_two(value):
    high = value.astype(BF)
    low = (value - high.astype(F32)).astype(BF)
    return high, low


def kernel(
    sizes,
    tokens, cotangent, routing, w_router, running_mean, w_gate, w_up, w_down,
    grad_tokens, grad_router, grad_gate, grad_up, grad_down,
    place, send_rows, in_rows, rows, wg, wu, wd,
    part, recv, full,
    sum_src, sum_in, sum_out, gr_src, gr_in, gr_out,
    top_src, top_parts, top_out,
    prob_ref, chosen_ref, w_send, w_in, dots_send, dots_in, dlog_hi, dlog_lo,
    back_send, back_in, out_gate, out_up, out_down,
    rows_s, rows_r, wx_s, wx_r, wl_s,
    p1_s, p1_r, p2_s, p2_r, p3_s, p3_r,
    rs_s, rs_r, ag_s, ag_r,
    wt_s, wt_r, dt_s, dt_r, bk_s, bk_r,
    ox_s, ox_r,
):
    NE, Z, E, TOK, H, W, CAP = sizes
    ND = Z * CORES
    NQ = NE * CORES
    S = NE // Z
    HZ = Z // 2
    HH = H // 2
    SC = S * CAP
    EL = 64
    GB = NE // (W // 128)
    PAIR = 2 * CAP
    ROWS = NE * CAP

    dp = lax.axis_index("dp")
    xy = lax.axis_index("expert")
    z = div(dp, CORES)
    c = rem(dp, CORES)
    other = 1 - c
    q = xy * CORES + c
    zr = rem(z + xy, Z)
    right = rem(z + 1, Z)
    left = rem(z + Z - 1, Z)
    twin = (z * CORES + other, xy)

    def plane_peer(q2):
        return (z * CORES + rem(q2, CORES), div(q2, CORES))

    def target(k):
        i, n = div(k, S * CORES), rem(k, S * CORES)
        distance = HZ + div(i + 1, 2) * (1 - 2 * rem(i, 2))
        owner = rem(div(xy, S) - z - distance + 2 * Z, Z) + div(n, CORES) * Z
        return owner * CORES + rem(c + n, CORES)

    def issue(which, first, last):
        def body(k):
            q2 = target(k)

            @pl.when(q2 != q)
            def _():
                rows_copy(which, q2).start()

        loop(first * S * CORES, last * S * CORES, body)

    def each_source(t, action):
        def body(n):
            q2 = t * (S * CORES) + n
            pl.when(q2 != q)(lambda: action(q2))

        loop(0, S * CORES, body)

    barrier = pltpu.get_barrier_semaphore()

    def greet_plane(k):
        pl.semaphore_signal(
            barrier, inc=1, device_id=plane_peer(rem(q + k, NQ)), device_id_type=MESH
        )

    def greet_column(m):
        z2 = rem(z + 1 + div(m, CORES), Z)
        pl.semaphore_signal(
            barrier, inc=1, device_id=(z2 * CORES + rem(m, CORES), xy), device_id_type=MESH
        )

    loop(1, NQ, greet_plane)
    loop(0, CORES * (Z - 1), greet_column)

    def own_weights(i, src, dst):
        return pltpu.make_async_copy(src, dst, wl_s.at[i])

    half = pl.ds(pl.multiple_of(c * W, W), W)
    mine = pl.ds(c * 2, 2)
    theirs = pl.ds(other * 2, 2)
    own_copies = [
        own_weights(0, w_gate.at[mine], wg.at[:, half, :]),
        own_weights(1, w_up.at[mine], wu.at[:, half, :]),
        own_weights(2, w_down.at[mine], wd.at[c]),
    ]
    for copy in own_copies:
        copy.start()

    route = routing[...]
    row_e = lax.broadcasted_iota(jnp.int32, (E, TOK), 0)
    has = jnp.zeros((E, TOK), F32)
    for k in range(route.shape[0]):
        has = has + jnp.where(route[k : k + 1, :] == row_e, 1.0, 0.0)
    t_row = lax.broadcasted_iota(jnp.int32, (TOK, TOK), 0)
    t_col = lax.broadcasted_iota(jnp.int32, (TOK, TOK), 1)
    before = jnp.where(t_row < t_col, 1.0, 0.0).astype(BF)
    same = jnp.where(t_row == t_col, 1.0, 0.0).astype(BF)
    pos = jnp.where(has > 0.5, dot_nn(has.astype(BF), before), -1.0)
    chosen_ref[...] = dot_nt(same, has.astype(BF))
    slot_iota = lax.broadcasted_iota(jnp.int32, (E, CAP, TOK), 1).astype(F32)
    placing = jnp.where(pos[:, None, :] == slot_iota, 1.0, 0.0)
    placing = placing.reshape(E * CAP, TOK).astype(BF)
    place[...] = placing.reshape(NE, CORES, PAIR, TOK)
    send_rows[0] = dot_nn(placing, tokens[...]).astype(BF).reshape(NQ, PAIR, W)
    send_rows[1] = dot_nn(placing, cotangent[...]).astype(BF).reshape(NQ, PAIR, W)

    pl.semaphore_wait(barrier, NQ - 1 + CORES * (Z - 1))

    def rows_copy(which, q2):
        return remote(
            send_rows.at[which, q2], in_rows.at[which, c, xy],
            rows_s.at[which, q2], rows_r.at[which, q], plane_peer(q2),
        )

    def rows_arrival(which, q2):
        return remote(
            send_rows.at[which, q2], in_rows.at[which, rem(q2, CORES), div(q2, CORES)],
            rows_s.at[which, q2], rows_r.at[which, q2], plane_peer(q2),
        )

    weight_copies = [
        remote(w_gate.at[theirs], wg.at[:, half, :], wx_s.at[0], wx_r.at[0], twin),
        remote(w_up.at[theirs], wu.at[:, half, :], wx_s.at[1], wx_r.at[1], twin),
        remote(w_down.at[theirs], wd.at[c], wx_s.at[2], wx_r.at[2], twin),
    ]
    other_half = pl.ds(pl.multiple_of(other * W, W), W)
    weight_arrivals = [
        remote(w_gate.at[theirs], wg.at[:, other_half, :], wx_s.at[0], wx_r.at[0], twin),
        remote(w_up.at[theirs], wu.at[:, other_half, :], wx_s.at[1], wx_r.at[1], twin),
        remote(w_down.at[theirs], wd.at[other], wx_s.at[2], wx_r.at[2], twin),
    ]
    weight_copies[0].start()
    weight_copies[1].start()
    issue(0, 0, ROWS_FIRST)
    in_rows[0, c, xy] = send_rows[0, q]
    in_rows[1, c, xy] = send_rows[1, q]

    def sum_blocks(n, index, peer, src, into, out, sem_s, sem_r):
        def scatter(j):
            return remote(src.at[j], into.at[index], sem_s.at[0, j], sem_r.at[0, index], peer(j))

        def scatter_arrival(j):
            return remote(src.at[j], into.at[j], sem_s.at[0, j], sem_r.at[0, j], peer(j))

        def gather(j):
            return remote(
                out.at[index], out.at[index], sem_s.at[1, j], sem_r.at[1, index], peer(j)
            )

        def gather_arrival(j):
            return remote(out.at[j], out.at[j], sem_s.at[1, j], sem_r.at[1, j], peer(j))

        def send():
            loop(1, n, lambda k: scatter(rem(index + k, n)).start())
            into[index] = src[index]

        def reduce():
            loop(1, n, lambda k: scatter_arrival(rem(index + k, n)).wait_recv())
            out[index] = jnp.sum(into[...], axis=0)
            loop(1, n, lambda k: gather(rem(index + k, n)).start())

        def finish():
            loop(1, n, lambda k: gather_arrival(rem(index + k, n)).wait_recv())

        def drain():
            loop(1, n, lambda k: scatter(rem(index + k, n)).wait_send())
            loop(1, n, lambda k: gather(rem(index + k, n)).wait_send())

        return send, reduce, finish, drain

    p1_send, p1_reduce, p1_finish, p1_drain = sum_blocks(
        ND, dp, lambda j: (j, xy), sum_src, sum_in, sum_out, p1_s, p1_r
    )
    p2_send, p2_reduce, p2_finish, p2_drain = sum_blocks(
        NE, xy, lambda j: (dp, j), gr_src, gr_in, gr_out, p2_s, p2_r
    )

    p3_send, p3_reduce, p3_finish, p3_drain = sum_blocks(
        ND, dp, lambda j: (j, xy), top_src, top_parts, top_out, p3_s, p3_r
    )

    def packed(first, second, count):
        if E < EL:
            gap = jnp.zeros((TOK, EL - E), F32)
            first = jnp.concatenate([first, gap], axis=1)
            second = jnp.concatenate([second, gap], axis=1)
        return jnp.concatenate([first, second], axis=1).reshape(count, TOK // count, 2 * EL)

    logits_part = dot_nt(tokens[...], w_router[...])
    mean_part = dot_nt(cotangent[...], running_mean[...])
    sum_src[...] = packed(logits_part, mean_part, ND)
    p1_send()

    def order_rows(which, t):
        each_source(t, lambda q2: rows_arrival(which, q2).wait_recv())
        at = pl.ds(pl.multiple_of(t * SC, SC), SC)
        for h in range(CORES):
            block = in_rows[which, h, pl.ds(t * S, S)].astype(F32)
            for j in range(2):
                piece = block[:, j * CAP : (j + 1) * CAP, :].reshape(SC, W)
                rows[which, j, at, h * W : (h + 1) * W] = piece.astype(BF)

    def some_rows(which, j, places):
        return jnp.concatenate(
            [rows[which, j, pl.ds(pl.multiple_of(t * SC, SC), SC), :] for t in places], axis=0
        )

    def forward_parts(*places, ordered=False):
        for t in places:
            if not ordered:
                order_rows(0, t)
        for j in range(2):
            x = some_rows(0, j, places)
            for r in range(2):
                cols = slice(r * HH, (r + 1) * HH)
                gate = dot_nn(x, wg[j, :, cols]).astype(BF)
                up = dot_nn(x, wu[j, :, cols]).astype(BF)
                for i, t in enumerate(places):
                    part[j, t, r, :, 0:HH] = gate[i * SC : (i + 1) * SC]
                    part[j, t, r, :, HH:H] = up[i * SC : (i + 1) * SC]

    def backward_parts(*places):
        for t in places:
            order_rows(1, t)
        for j in range(2):
            x = some_rows(1, j, places)
            for r in range(2):
                units = slice(r * HH, (r + 1) * HH)
                value = dot_nt(x[:, 0:W], wd[0, j, units, :]) + dot_nt(
                    x[:, W : 2 * W], wd[1, j, units, :]
                )
                value = value.astype(BF)
                for i, t in enumerate(places):
                    part[2, t, r, :, j * HH : (j + 1) * HH] = value[i * SC : (i + 1) * SC]

    def ring_peer(r):
        return ((right if r == 0 else left) * CORES + c, xy)

    def rs_copy(k, r, s):
        t = rem(zr + HZ - s, Z) if r == 0 else rem(zr - HZ + s + Z, Z)
        if s == 0:
            src, dst = part.at[k, t, r], recv.at[k, r, 0, r]
        else:
            src, dst = part.at[k, t], recv.at[k, r, s]
        return remote(src, dst, rs_s.at[k, r, s], rs_r.at[k, r, s], ring_peer(r))

    def rs_step(k, s):
        for r in range(2):
            rs_copy(k, r, s).wait_recv()
            t = rem(zr + HZ - s - 1, Z) if r == 0 else rem(zr - HZ + s + 1 + Z, Z)
            if s == 0:
                part[k, t, r] = (part[k, t, r].astype(F32) + recv[k, r, 0, r].astype(F32)).astype(BF)
            else:
                part[k, t] = (part[k, t].astype(F32) + recv[k, r, s].astype(F32)).astype(BF)
            rs_copy(k, r, s + 1).start()

    def rs_start(k):
        for r in range(2):
            rs_copy(k, r, 0).start()

    def rs_end(k):
        for r in range(2):
            rs_copy(k, r, HZ - 1).wait_recv()

    def ag_copy(k, r, s):
        t = rem(zr - s + Z, Z) if r == 0 else rem(zr + s, Z)
        ref = full.at[k, t, r] if s == HZ - 1 else full.at[k, t]
        return remote(ref, ref, ag_s.at[k, r, s], ag_r.at[k, r, s], ring_peer(r))

    def ag_arrival(k, r, s):
        t = rem(zr - 1 - s + Z, Z) if r == 0 else rem(zr + 1 + s, Z)
        ref = full.at[k, t, r] if s == HZ - 1 else full.at[k, t]
        return remote(ref, ref, ag_s.at[k, r, s], ag_r.at[k, r, s], ring_peer(r))

    def ag_step(k, s):
        for r in range(2):
            ag_arrival(k, r, s).wait_recv()
            if s < HZ - 1:
                ag_copy(k, r, s + 1).start()

    def ag_start(k):
        for r in range(2):
            ag_copy(k, r, 0).start()

    def two_places(distance):
        return rem(zr + distance, Z), rem(zr - distance + Z, Z)

    def backward_start():
        own_copies[2].wait()
        weight_arrivals[2].wait_recv()
        backward_parts(rem(zr + HZ, Z))
        rs_start(2)

    own_copies[0].wait()
    own_copies[1].wait()
    weight_arrivals[0].wait_recv()
    weight_arrivals[1].wait_recv()
    order_rows(0, rem(zr + HZ, Z))
    issue(0, ROWS_FIRST, Z)
    weight_copies[2].start()
    issue(1, 0, GRADS_FIRST)
    forward_parts(rem(zr + HZ, Z), ordered=True)
    rs_start(0)
    rs_start(1)
    p1_reduce()
    for s in range(HZ - 1):
        forward_parts(*two_places(HZ - 1 - s))
        for j in range(2):
            rs_step(j, s)
        if s == 0:
            issue(1, GRADS_FIRST, GRADS_NEXT)
        if s == max(HZ - 3, 0):
            issue(1, GRADS_NEXT, Z)
            backward_start()
    forward_parts(zr)
    backward_parts(*two_places(HZ - 1))
    rs_step(2, 0)

    p1_finish()
    sums = sum_out[...].reshape(TOK, 2 * EL)
    weights_exp = jnp.exp(sums[:, 0:E])
    prob_ref[...] = weights_exp / jnp.sum(weights_exp, axis=1, keepdims=True)

    spot = rem(xy, S)
    first_owner = rem(div(xy, S) - z + Z, Z)
    owners = [first_owner + m * Z for m in range(S)]
    pair_row = lax.broadcasted_iota(jnp.int32, (PAIR, 2 * EL), 0)
    pair_lane = lax.broadcasted_iota(jnp.int32, (PAIR, 2 * EL), 1)
    pair_expert = c * 2 + jnp.where(pair_row >= CAP, 1, 0)

    def w_copy(m):
        return remote(
            w_send.at[m], w_in.at[spot], wt_s.at[m], wt_r.at[spot], (dp, owners[m])
        )

    def w_arrival(b):
        return remote(w_send.at[b], w_in.at[b], wt_s.at[b], wt_r.at[b], (dp, zr * S + b))

    for m in range(S):
        spread = dot_nn(place[owners[m], c], prob_ref[...].astype(BF))
        if E < 2 * EL:
            spread = jnp.concatenate([spread, jnp.zeros((PAIR, 2 * EL - E), F32)], axis=1)
        spread = jnp.where(pair_lane == owners[m] * 4 + pair_expert, spread, 0.0)
        column = jnp.sum(spread, axis=1, keepdims=True)
        w_send[m] = jnp.broadcast_to(column, (PAIR, 2 * EL)).astype(BF)

        @pl.when(owners[m] != xy)
        def _(m=m):
            w_copy(m).start()

        @pl.when(owners[m] == xy)
        def _(m=m):
            w_in[spot] = w_send[m]

    for s in range(1, HZ - 1):
        backward_parts(*two_places(HZ - 1 - s))
        rs_step(2, s)
    backward_parts(zr)

    for b in range(S):

        @pl.when(zr * S + b != xy)
        def _(b=b):
            w_arrival(b).wait_recv()

    for k in range(3):
        rs_end(k)

    def total(k, r, cols):
        value = part[k, zr, r, :, cols].astype(F32)
        return (
            value
            + recv[k, 0, HZ - 1, r, :, cols].astype(F32)
            + recv[k, 1, HZ - 1, r, :, cols].astype(F32)
        )

    dots = []
    for j in range(2):
        weight = jnp.concatenate(
            [w_in[b].astype(F32)[j * CAP : (j + 1) * CAP, 0:1] for b in range(S)], axis=0
        )
        dot = jnp.zeros((SC, 1), F32)
        for r in range(2):
            cols = slice(j * HH, (j + 1) * HH)
            raw = total(2, r, cols)
            gate = total(j, r, slice(0, HH))
            up = total(j, r, slice(HH, H))
            sig = 1.0 / (1.0 + jnp.exp(-gate))
            silu = gate * sig
            hidden = silu * up
            d_hidden = raw * weight
            full[j, zr, r, :, 0:HH] = (
                d_hidden * up * sig * (1.0 + gate * (1.0 - sig))
            ).astype(BF)
            full[j, zr, r, :, HH:H] = (d_hidden * silu).astype(BF)
            full[2, zr, r, :, cols] = (hidden * weight).astype(BF)
            dot = dot + jnp.sum(hidden * raw, axis=1, keepdims=True)
        ag_start(j)
        dots.append(dot)
    ag_start(2)

    def dots_copy(b):
        return remote(
            dots_send.at[b], dots_in.at[div(xy, Z)], dt_s.at[b], dt_r.at[div(xy, Z)], (dp, zr * S + b)
        )

    def dots_arrival(m):
        return remote(dots_send.at[m], dots_in.at[m], dt_s.at[m], dt_r.at[m], (dp, owners[m]))

    for b in range(S):
        value = jnp.concatenate(
            [dots[0][b * CAP : (b + 1) * CAP], dots[1][b * CAP : (b + 1) * CAP]], axis=0
        )
        value = jnp.broadcast_to(value, (PAIR, 2 * EL))
        high = value.astype(BF).astype(F32)
        dots_send[b] = jnp.where(pair_lane < EL, high, value - high).astype(BF)

        @pl.when(zr * S + b != xy)
        def _(b=b):
            dots_copy(b).start()

        @pl.when(zr * S + b == xy)
        def _(b=b):
            dots_in[div(xy, Z)] = dots_send[b]

    def back_copy(q2):
        return remote(
            back_send.at[div(q2, CORES), rem(q2, CORES)], back_in.at[q],
            bk_s.at[q2], bk_r.at[q], plane_peer(q2),
        )

    def back_arrival(q2):
        return remote(
            back_send.at[div(q2, CORES), rem(q2, CORES)], back_in.at[q2],
            bk_s.at[q2], bk_r.at[q2], plane_peer(q2),
        )

    def send_back(*places):
        values = []
        for j in range(2):
            value = None
            for r in range(2):
                cols = slice(r * HH, (r + 1) * HH)
                both = jnp.concatenate([full[j, t, r] for t in places], axis=0)
                term = dot_nt(both[:, 0:HH], wg[j, :, cols]) + dot_nt(
                    both[:, HH:H], wu[j, :, cols]
                )
                value = term if value is None else value + term
            values.append(value)
        for i, t in enumerate(places):
            for b in range(S):
                at = slice(i * SC + b * CAP, i * SC + (b + 1) * CAP)
                block = jnp.concatenate([values[0][at], values[1][at]], axis=0).astype(BF)
                for h in range(CORES):
                    source = t * S + b
                    q2 = source * CORES + h
                    back_send[source, h] = block[:, h * W : (h + 1) * W]

                    @pl.when(q2 != q)
                    def _(q2=q2):
                        back_copy(q2).start()

                    @pl.when(q2 == q)
                    def _(source=source, h=h):
                        back_in[q] = back_send[source, h]

    def send_dots():
        for m in range(S):

            @pl.when(owners[m] != xy)
            def _(m=m):
                dots_arrival(m).wait_recv()

        top = None
        for m in range(S):
            lane_e = jnp.where(pair_lane >= EL, pair_lane - EL, pair_lane)
            masked = jnp.where(
                lane_e == owners[m] * 4 + pair_expert, dots_in[m].astype(F32), 0.0
            ).astype(BF)
            term = dot_tn(place[owners[m], c], masked)
            top = term if top is None else top + term
        top_src[...] = top.reshape(ND, TOK // ND, 2 * EL)
        p3_send()

    def router_gradients():
        p3_finish()
        top = top_out[...].reshape(TOK, 2 * EL)
        top = top[:, 0:E] + top[:, EL : EL + E]
        mean = sum_out[...].reshape(TOK, 2 * EL)[:, EL : EL + E]
        d_prob = jnp.where(chosen_ref[...] > 0.5, top, mean)
        prob = prob_ref[...]
        dlogits = prob * (d_prob - jnp.sum(prob * d_prob, axis=1, keepdims=True))
        high, low = split_two(dlogits)
        dlog_hi[...] = high
        dlog_lo[...] = low
        router_part = dot_tn(high, tokens[...]) + dot_tn(low, tokens[...])
        for h in range(W // 128):
            gr_src[h * GB : (h + 1) * GB] = router_part[:, h * 128 : (h + 1) * 128].reshape(
                GB, E // GB, 128
            )
        p2_send()

    actions = [send_dots, p3_reduce, router_gradients, p2_reduce]
    send_back(zr)
    for s in range(HZ):
        for j in range(2):
            ag_step(j, s)
        if s < HZ - 1:
            send_back(*two_places(1 + s))
            ag_step(2, s)
            actions[s]()
        else:
            send_back(rem(zr + HZ, Z))
            for action in actions[s:]:
                action()

    def give(i, j):
        out = (grad_gate, grad_up, grad_down)[i]
        buf = (out_gate, out_up, out_down)[i]
        return remote(
            buf.at[j], out.at[c * 2 + j], ox_s.at[i, j], ox_r.at[i, j], twin
        )

    def take(i, j):
        out = (grad_gate, grad_up, grad_down)[i]
        buf = (out_gate, out_up, out_down)[i]
        return remote(
            buf.at[j], out.at[other * 2 + j], ox_s.at[i, j], ox_r.at[i, j], twin
        )

    for mine_now in (False, True):
        features = half if mine_now else other_half
        for j in range(2):
            x = rows[0, j, :, features]
            for r in range(2):
                cols = slice(r * HH, (r + 1) * HH)
                both = full[j, :, r].reshape(ROWS, H)
                gate = dot_tn(x, both[:, 0:HH]).astype(BF)
                up = dot_tn(x, both[:, HH:H]).astype(BF)
                if mine_now:
                    grad_gate[c * 2 + j, :, cols] = gate
                    grad_up[c * 2 + j, :, cols] = up
                else:
                    out_gate[j, :, cols] = gate
                    out_up[j, :, cols] = up
            if not mine_now:
                give(0, j).start()
                give(1, j).start()
        if not mine_now:
            ag_step(2, HZ - 1)
        for j in range(2):
            x = rows[1, j, :, features]
            for r in range(2):
                units = slice(r * HH, (r + 1) * HH)
                hid = full[2, :, r, :, j * HH : (j + 1) * HH].reshape(ROWS, HH)
                down = dot_tn(hid, x).astype(BF)
                if mine_now:
                    grad_down[c * 2 + j, units, :] = down
                else:
                    out_down[j, units, :] = down
            if not mine_now:
                give(2, j).start()

    loop(1, NQ, lambda k: back_arrival(rem(q + k, NQ)).wait_recv())
    router_term = dot_nn(dlog_hi[...], w_router[...]) + dot_nn(dlog_lo[...], w_router[...])
    token_term = dot_tn(
        place[...].reshape(E * CAP, TOK), back_in[...].reshape(E * CAP, W)
    )
    grad_tokens[...] = (token_term + router_term).astype(BF)
    p2_finish()
    for h in range(W // 128):
        grad_router[:, h * 128 : (h + 1) * 128] = gr_out[h * GB : (h + 1) * GB].reshape(E, 128)

    loop(1, NQ, lambda k: rows_copy(0, rem(q + k, NQ)).wait_send())
    loop(1, NQ, lambda k: rows_copy(1, rem(q + k, NQ)).wait_send())
    loop(1, NQ, lambda k: back_copy(rem(q + k, NQ)).wait_send())
    for copy in weight_copies:
        copy.wait_send()
    p1_drain()
    p2_drain()
    p3_drain()

    for k in range(3):
        for r in range(2):
            for s in range(HZ):
                rs_copy(k, r, s).wait_send()
                ag_copy(k, r, s).wait_send()

    for m in range(S):

        @pl.when(owners[m] != xy)
        def _(m=m):
            w_copy(m).wait_send()

    for b in range(S):

        @pl.when(zr * S + b != xy)
        def _(b=b):
            dots_copy(b).wait_send()

    for i in range(3):
        for j in range(2):
            give(i, j).wait_send()
            take(i, j).wait_recv()


def per_device(tokens, cotangent, routing, w_router, running_mean, w_gate, w_up, w_down):
    NE = lax.axis_size("expert")
    ND = lax.axis_size("dp")
    Z = ND // CORES
    local_count, W, H = w_gate.shape
    E = NE * local_count
    TOK, top = routing.shape
    routing, w_router = routing.T, w_router.T
    CAP = 3 * TOK * top // (2 * E)
    NQ = NE * CORES
    S = NE // Z
    HZ = Z // 2
    PAIR, ROWS = 2 * CAP, NE * CAP
    sizes = (NE, Z, E, TOK, H, W, CAP)
    vmem = pl.BlockSpec(memory_space=pltpu.VMEM)
    hbm = pl.BlockSpec(memory_space=pl.ANY)
    dma = pltpu.SemaphoreType.DMA
    scratch = [
        pltpu.VMEM((NE, CORES, PAIR, TOK), BF),
        pltpu.VMEM((2, NQ, PAIR, W), BF),
        pltpu.VMEM((2, CORES, NE, PAIR, W), BF),
        pltpu.VMEM((2, 2, ROWS, 2 * W), BF),
        pltpu.VMEM((2, 2 * W, H), BF),
        pltpu.VMEM((2, 2 * W, H), BF),
        pltpu.VMEM((2, 2, H, W), BF),
        pltpu.VMEM((3, Z, 2, S * CAP, H), BF),
        pltpu.VMEM((3, 2, HZ, 2, S * CAP, H), BF),
        pltpu.VMEM((3, Z, 2, S * CAP, H), BF),
        pltpu.VMEM((ND, TOK // ND, 128), F32),
        pltpu.VMEM((ND, TOK // ND, 128), F32),
        pltpu.VMEM((ND, TOK // ND, 128), F32),
        pltpu.VMEM((NE, E * W // (128 * NE), 128), F32),
        pltpu.VMEM((NE, E * W // (128 * NE), 128), F32),
        pltpu.VMEM((NE, E * W // (128 * NE), 128), F32),
        pltpu.VMEM((ND, TOK // ND, 128), F32),
        pltpu.VMEM((ND, TOK // ND, 128), F32),
        pltpu.VMEM((ND, TOK // ND, 128), F32),
        pltpu.VMEM((TOK, E), F32),
        pltpu.VMEM((TOK, E), F32),
        pltpu.VMEM((S, PAIR, 128), BF),
        pltpu.VMEM((S, PAIR, 128), BF),
        pltpu.VMEM((S, PAIR, 128), BF),
        pltpu.VMEM((S, PAIR, 128), BF),
        pltpu.VMEM((TOK, E), BF),
        pltpu.VMEM((TOK, E), BF),
        pltpu.VMEM((NE, CORES, PAIR, W), BF),
        pltpu.VMEM((NQ, PAIR, W), BF),
        pltpu.VMEM((2, W, H), BF),
        pltpu.VMEM((2, W, H), BF),
        pltpu.VMEM((2, H, W), BF),
        dma((2, NQ)), dma((2, NQ)),
        dma((3,)), dma((3,)), dma((3,)),
        dma((2, ND)), dma((2, ND)),
        dma((2, NE)), dma((2, NE)),
        dma((2, ND)), dma((2, ND)),
        dma((3, 2, HZ)), dma((3, 2, HZ)),
        dma((3, 2, HZ)), dma((3, 2, HZ)),
        dma((S,)), dma((S,)),
        dma((S,)), dma((S,)),
        dma((NQ,)), dma((NQ,)),
        dma((3, 2)), dma((3, 2)),
    ]
    results = pl.pallas_call(
        functools.partial(kernel, sizes),
        out_shape=(
            pltpu.VMEM((TOK, W), BF),
            pltpu.VMEM((E, W), F32),
            pltpu.VMEM((local_count, W, H), BF),
            pltpu.VMEM((local_count, W, H), BF),
            pltpu.VMEM((local_count, H, W), BF),
        ),
        in_specs=[vmem] * 5 + [hbm] * 3,
        out_specs=(vmem, vmem, vmem, vmem, vmem),
        scratch_shapes=scratch,
        compiler_params=pltpu.CompilerParams(
            collective_id=0, has_side_effects=True, vmem_limit_bytes=56 * 1024 * 1024
        ),
        cost_estimate=pl.CostEstimate(
            flops=6 * 10**9, bytes_accessed=10**7, transcendentals=10**5
        ),
    )(tokens, cotangent, routing, w_router, running_mean, w_gate, w_up, w_down)
    grad_tokens, grad_router, *rest = results
    return (grad_tokens, grad_router.T, *rest)


def solution(mesh):
    return jax.shard_map(
        per_device,
        mesh=mesh,
        in_specs=(
            P("expert", "dp"),
            P("expert", "dp"),
            P("expert", None),
            P("dp", None),
            P(None, "dp"),
            P("expert", "dp", None),
            P("expert", "dp", None),
            P("expert", None, "dp"),
        ),
        out_specs=(
            P("expert", "dp"),
            P("dp", None),
            P("expert", "dp", None),
            P("expert", "dp", None),
            P("expert", None, "dp"),
        ),
        check_vma=False,
    )
```

```python
import functools

import jax
import jax.numpy as jnp
from jax import lax
from jax.experimental import pallas as pl
from jax.experimental.pallas import tpu as pltpu
from jax.sharding import PartitionSpec as P

MESH = pl.DeviceIdType.MESH
BF = jnp.bfloat16
F32 = jnp.float32
CORES = 2
ROWS_FIRST = 3
ROWS_NEXT = 8
GRADS_FIRST = 1
GRADS_NEXT = 4
BACK_AT = 0


def rem(a, n):
    return lax.rem(a, jnp.int32(n))


def div(a, n):
    return lax.div(a, jnp.int32(n))


def remote(src, dst, send_sem, recv_sem, device):
    return pltpu.make_async_remote_copy(
        src_ref=src,
        dst_ref=dst,
        send_sem=send_sem,
        recv_sem=recv_sem,
        device_id=device,
        device_id_type=MESH,
    )


def loop(lower, upper, body):
    def step(i, carry):
        body(i)
        return carry

    lax.fori_loop(lower, upper, step, 0)


def dot_nn(a, b):
    return jnp.dot(a, b, preferred_element_type=F32)


def dot_nt(a, b):
    return lax.dot_general(a, b, (((1,), (1,)), ((), ())), preferred_element_type=F32)


def dot_tn(a, b):
    return lax.dot_general(a, b, (((0,), (0,)), ((), ())), preferred_element_type=F32)


def split_two(value):
    high = value.astype(BF)
    low = (value - high.astype(F32)).astype(BF)
    return high, low


def kernel(
    sizes,
    tokens, cotangent, routing, w_router, running_mean, w_gate, w_up, w_down,
    grad_tokens, grad_router, grad_gate, grad_up, grad_down,
    place, send_rows, in_rows, rows, wg, wu, wd,
    part, recv, full, part_b, recv_b, full_b,
    sum_src, sum_in, sum_out, gr_src, gx_in, gy_in, gr_out, top_in,
    prob_ref, chosen_ref, w_send, w_in, dots_send, dots_in, dlog_hi, dlog_lo,
    back_send, back_in, out_gate, out_up, out_down,
    rows_s, rows_r, wx_s, wx_r, wl_s,
    p1_s, p1_r, p2_s, p2_r, tp_s, tp_r,
    rs_s, rs_r, ag_s, ag_r,
    wt_s, wt_r, dt_s, dt_r, bk_s, bk_r,
    ox_s, ox_r,
):
    NE, Z, E, TOK, H, W, CAP = sizes
    ND = Z * CORES
    NQ = NE * CORES
    S = NE // Z
    HZ = Z // 2
    HH = H // 2
    SC = S * CAP
    EL = 64
    PAIR = 2 * CAP
    ROWS = NE * CAP

    dp = lax.axis_index("dp")
    xy = lax.axis_index("expert")
    z = div(dp, CORES)
    c = rem(dp, CORES)
    other = 1 - c
    q = xy * CORES + c
    zr = rem(z + xy, Z)
    right = rem(z + 1, Z)
    left = rem(z + Z - 1, Z)
    twin = (z * CORES + other, xy)

    def in_plane(owner, core):
        return (z * CORES + core, owner)

    cores = (c, other)

    def each_target(i, action):
        distance = HZ + div(i + 1, 2) * (1 - 2 * rem(i, 2))
        first = rem(div(xy, S) - z - distance + 2 * Z, Z)
        for m in range(S):
            owner = first + m * Z
            for core in cores:
                if core is c:
                    pl.when(owner != xy)(lambda owner=owner, core=core: action(owner, core))
                else:
                    action(owner, core)

    def issue(which, first, last):
        loop(
            first,
            last,
            lambda i: each_target(i, lambda o, h: rows_copy(which, o, h).start()),
        )

    def each_source(t, action):
        for b in range(S):
            source = t * S + b
            for core in cores:
                if core is c:
                    pl.when(source != xy)(lambda source=source, core=core: action(source, core))
                else:
                    action(source, core)

    barrier = pltpu.get_barrier_semaphore()

    def greet(*device):
        pl.semaphore_signal(barrier, inc=1, device_id=device, device_id_type=MESH)

    def greet_plane(k):
        for core in range(CORES):
            greet(z * CORES + core, rem(xy + k, NE))

    def greet_column(k):
        for core in range(CORES):
            greet(rem(z + k, Z) * CORES + core, xy)

    greet(*twin)
    loop(1, NE, greet_plane)
    loop(1, Z, greet_column)

    def own_weights(i, src, dst):
        return pltpu.make_async_copy(src, dst, wl_s.at[i])

    half = pl.ds(pl.multiple_of(c * W, W), W)
    mine = pl.ds(c * 2, 2)
    theirs = pl.ds(other * 2, 2)
    own_copies = [
        own_weights(0, w_gate.at[mine], wg.at[:, half, :]),
        own_weights(1, w_up.at[mine], wu.at[:, half, :]),
        own_weights(2, w_down.at[mine], wd.at[c]),
    ]
    for copy in own_copies:
        copy.start()

    route = routing[...]
    row_e = lax.broadcasted_iota(jnp.int32, (E, TOK), 0)
    has = jnp.zeros((E, TOK), F32)
    for k in range(route.shape[0]):
        has = has + jnp.where(route[k : k + 1, :] == row_e, 1.0, 0.0)
    t_row = lax.broadcasted_iota(jnp.int32, (TOK, TOK), 0)
    t_col = lax.broadcasted_iota(jnp.int32, (TOK, TOK), 1)
    before = jnp.where(t_row < t_col, 1.0, 0.0).astype(BF)
    same = jnp.where(t_row == t_col, 1.0, 0.0).astype(BF)
    pos = jnp.where(has > 0.5, dot_nn(has.astype(BF), before), -1.0)
    chosen_ref[...] = dot_nt(same, has.astype(BF))
    slot_iota = lax.broadcasted_iota(jnp.int32, (E, CAP, TOK), 1).astype(F32)
    placing = jnp.where(pos[:, None, :] == slot_iota, 1.0, 0.0)
    placing = placing.reshape(E * CAP, TOK).astype(BF)
    place[...] = placing.reshape(NE, CORES, PAIR, TOK)
    send_rows[0] = dot_nn(placing, tokens[...]).astype(BF).reshape(NQ, PAIR, W)
    send_rows[1] = dot_nn(placing, cotangent[...]).astype(BF).reshape(NQ, PAIR, W)

    pl.semaphore_wait(barrier, NQ - 1 + CORES * (Z - 1))

    def rows_copy(which, owner, core):
        q2 = owner * CORES + core
        return remote(
            send_rows.at[which, q2], in_rows.at[which, c, xy],
            rows_s.at[which, q2], rows_r.at[which, q], in_plane(owner, core),
        )

    def rows_arrival(which, source, core):
        q2 = source * CORES + core
        return remote(
            send_rows.at[which, q2], in_rows.at[which, core, source],
            rows_s.at[which, q2], rows_r.at[which, q2], in_plane(source, core),
        )

    weight_copies = [
        remote(w_gate.at[theirs], wg.at[:, half, :], wx_s.at[0], wx_r.at[0], twin),
        remote(w_up.at[theirs], wu.at[:, half, :], wx_s.at[1], wx_r.at[1], twin),
        remote(w_down.at[theirs], wd.at[c], wx_s.at[2], wx_r.at[2], twin),
    ]
    other_half = pl.ds(pl.multiple_of(other * W, W), W)
    weight_arrivals = [
        remote(w_gate.at[theirs], wg.at[:, other_half, :], wx_s.at[0], wx_r.at[0], twin),
        remote(w_up.at[theirs], wu.at[:, other_half, :], wx_s.at[1], wx_r.at[1], twin),
        remote(w_down.at[theirs], wd.at[other], wx_s.at[2], wx_r.at[2], twin),
    ]
    weight_copies[0].start()
    weight_copies[1].start()
    issue(0, 0, ROWS_FIRST)
    in_rows[0, c, xy] = send_rows[0, q]
    in_rows[1, c, xy] = send_rows[1, q]

    def sum_blocks(n, index, peer, src, into, out, sem_s, sem_r):
        def scatter(j):
            return remote(src.at[j], into.at[index], sem_s.at[0, j], sem_r.at[0, index], peer(j))

        def scatter_arrival(j):
            return remote(src.at[j], into.at[j], sem_s.at[0, j], sem_r.at[0, j], peer(j))

        def gather(j):
            return remote(
                out.at[index], out.at[index], sem_s.at[1, j], sem_r.at[1, index], peer(j)
            )

        def gather_arrival(j):
            return remote(out.at[j], out.at[j], sem_s.at[1, j], sem_r.at[1, j], peer(j))

        def send():
            loop(1, n, lambda k: scatter(rem(index + k, n)).start())
            into[index] = src[index]

        def reduce():
            loop(1, n, lambda k: scatter_arrival(rem(index + k, n)).wait_recv())
            out[index] = jnp.sum(into[...], axis=0)
            loop(1, n, lambda k: gather(rem(index + k, n)).start())

        def finish():
            loop(1, n, lambda k: gather_arrival(rem(index + k, n)).wait_recv())

        def drain():
            loop(1, n, lambda k: scatter(rem(index + k, n)).wait_send())
            loop(1, n, lambda k: gather(rem(index + k, n)).wait_send())

        return send, reduce, finish, drain

    p1_send, p1_reduce, p1_finish, p1_drain = sum_blocks(
        ND, dp, lambda j: (j, xy), sum_src, sum_in, sum_out, p1_s, p1_r
    )
    side = 4 if NE % 4 == 0 else NE
    x, y, NY = rem(xy, side), div(xy, side), NE // side

    def gx_copy(j):
        return remote(
            gr_src.at[j], gx_in.at[x], p2_s.at[0, j], p2_r.at[0, x], (dp, y * side + j)
        )

    def gx_arrival(j):
        return remote(
            gr_src.at[j], gx_in.at[j], p2_s.at[0, j], p2_r.at[0, j], (dp, y * side + j)
        )

    def gy_copy(j):
        return remote(
            gy_in.at[y], gy_in.at[y], p2_s.at[1, j], p2_r.at[1, y], (dp, j * side + x)
        )

    def gy_arrival(j):
        return remote(
            gy_in.at[j], gy_in.at[j], p2_s.at[1, j], p2_r.at[1, j], (dp, j * side + x)
        )

    def gz_copy(j):
        return remote(
            gr_out.at[x], gr_out.at[x], p2_s.at[2, j], p2_r.at[2, x], (dp, y * side + j)
        )

    def gz_arrival(j):
        return remote(
            gr_out.at[j], gr_out.at[j], p2_s.at[2, j], p2_r.at[2, j], (dp, y * side + j)
        )

    def p2_send():
        for k in range(1, side):
            gx_copy(rem(x + k, side)).start()
        gx_in[x] = gr_src[x]

    def p2_middle():
        for k in range(1, side):
            gx_arrival(rem(x + k, side)).wait_recv()
        gy_in[y] = jnp.sum(gx_in[...], axis=0)
        for k in range(1, NY):
            gy_copy(rem(y + k, NY)).start()

    def p2_reduce():
        for k in range(1, NY):
            gy_arrival(rem(y + k, NY)).wait_recv()
        gr_out[x] = jnp.sum(gy_in[...], axis=0)
        for k in range(1, side):
            gz_copy(rem(x + k, side)).start()

    def p2_finish():
        for k in range(1, side):
            gz_arrival(rem(x + k, side)).wait_recv()

    def p2_drain():
        for k in range(1, side):
            gx_copy(rem(x + k, side)).wait_send()
            gz_copy(rem(x + k, side)).wait_send()
        for k in range(1, NY):
            gy_copy(rem(y + k, NY)).wait_send()

    def packed(first, second, count):
        if E < EL:
            gap = jnp.zeros((TOK, EL - E), F32)
            first = jnp.concatenate([first, gap], axis=1)
            second = jnp.concatenate([second, gap], axis=1)
        return jnp.concatenate([first, second], axis=1).reshape(count, TOK // count, 2 * EL)

    logits_part = dot_nt(tokens[...], w_router[...])
    mean_part = dot_nt(cotangent[...], running_mean[...])
    sum_src[...] = packed(logits_part, mean_part, ND)
    p1_send()

    def order_rows(which, t):
        each_source(t, lambda o, h: rows_arrival(which, o, h).wait_recv())
        at = pl.ds(pl.multiple_of(t * SC, SC), SC)
        for h in range(CORES):
            block = in_rows[which, h, pl.ds(t * S, S)].astype(F32)
            for j in range(2):
                piece = block[:, j * CAP : (j + 1) * CAP, :].reshape(SC, W)
                rows[which, j, at, h * W : (h + 1) * W] = piece.astype(BF)

    def some_rows(which, j, places):
        return jnp.concatenate(
            [rows[which, j, pl.ds(pl.multiple_of(t * SC, SC), SC), :] for t in places], axis=0
        )

    def forward_parts(*places, ordered=False):
        for t in places:
            if not ordered:
                order_rows(0, t)
        for j in range(2):
            some = some_rows(0, j, places)
            for r in range(2):
                cols = slice(r * HH, (r + 1) * HH)
                gate = dot_nn(some, wg[j, :, cols]).astype(BF)
                up = dot_nn(some, wu[j, :, cols]).astype(BF)
                for i, t in enumerate(places):
                    part[j, t, r, :, 0:HH] = gate[i * SC : (i + 1) * SC]
                    part[j, t, r, :, HH:H] = up[i * SC : (i + 1) * SC]

    def backward_parts(*places):
        for t in places:
            order_rows(1, t)
        for j in range(2):
            some = some_rows(1, j, places)
            for r in range(2):
                units = slice(r * HH, (r + 1) * HH)
                value = dot_nt(some[:, 0:W], wd[0, j, units, :]) + dot_nt(
                    some[:, W : 2 * W], wd[1, j, units, :]
                )
                value = value.astype(BF)
                for i, t in enumerate(places):
                    part_b[j, t, r] = value[i * SC : (i + 1) * SC]

    def ring_peer(r):
        return ((right if r == 0 else left) * CORES + c, xy)

    def sums_of(k):
        return (part.at[k], recv.at[k]) if k < 2 else (part_b.at[k - 2], recv_b.at[k - 2])

    def gathered(k):
        return full.at[k] if k < 2 else full_b.at[k - 2]

    def rs_copy(k, r, s):
        t = rem(zr + HZ - s, Z) if r == 0 else rem(zr - HZ + s + Z, Z)
        own, got = sums_of(k)
        if s == 0:
            src, dst = own.at[t, r], got.at[r, 0, r]
        else:
            src, dst = own.at[t], got.at[r, s]
        return remote(src, dst, rs_s.at[k, r, s], rs_r.at[k, r, s], ring_peer(r))

    def rs_step(k, s):
        own, got = sums_of(k)
        for r in range(2):
            rs_copy(k, r, s).wait_recv()
            t = rem(zr + HZ - s - 1, Z) if r == 0 else rem(zr - HZ + s + 1 + Z, Z)
            if s == 0:
                own[t, r] = (own[t, r].astype(F32) + got[r, 0, r].astype(F32)).astype(BF)
            else:
                own[t] = (own[t].astype(F32) + got[r, s].astype(F32)).astype(BF)
            rs_copy(k, r, s + 1).start()

    def rs_start(k):
        for r in range(2):
            rs_copy(k, r, 0).start()

    def rs_end(k):
        for r in range(2):
            rs_copy(k, r, HZ - 1).wait_recv()

    def ag_copy(k, r, s):
        t = rem(zr - s + Z, Z) if r == 0 else rem(zr + s, Z)
        ref = gathered(k).at[t, r] if s == HZ - 1 else gathered(k).at[t]
        return remote(ref, ref, ag_s.at[k, r, s], ag_r.at[k, r, s], ring_peer(r))

    def ag_arrival(k, r, s):
        t = rem(zr - 1 - s + Z, Z) if r == 0 else rem(zr + 1 + s, Z)
        ref = gathered(k).at[t, r] if s == HZ - 1 else gathered(k).at[t]
        return remote(ref, ref, ag_s.at[k, r, s], ag_r.at[k, r, s], ring_peer(r))

    def ag_step(k, s):
        for r in range(2):
            ag_arrival(k, r, s).wait_recv()
            if s < HZ - 1:
                ag_copy(k, r, s + 1).start()

    def ag_start(k):
        for r in range(2):
            ag_copy(k, r, 0).start()

    def two_places(distance):
        return rem(zr + distance, Z), rem(zr - distance + Z, Z)

    def backward_start():
        own_copies[2].wait()
        weight_arrivals[2].wait_recv()
        backward_parts(rem(zr + HZ, Z))
        rs_start(2)
        rs_start(3)

    own_copies[0].wait()
    own_copies[1].wait()
    weight_arrivals[0].wait_recv()
    weight_arrivals[1].wait_recv()
    order_rows(0, rem(zr + HZ, Z))
    issue(0, ROWS_FIRST, ROWS_NEXT)
    weight_copies[2].start()
    issue(1, 0, GRADS_FIRST)
    forward_parts(rem(zr + HZ, Z), ordered=True)
    rs_start(0)
    forward_parts(*two_places(HZ - 1))
    rs_start(1)
    back_at = min(BACK_AT, HZ - 2)
    for s in range(HZ - 1):
        if s > 0:
            forward_parts(*two_places(HZ - 1 - s))
        rs_step(0, s)
        if s > back_at:
            backward_parts(*two_places(HZ - 1 - (s - back_at - 1)))
            rs_step(2, s - back_at - 1)
            rs_step(3, s - back_at - 1)
        rs_step(1, s)
        if s == 0:
            p1_reduce()
            issue(0, ROWS_NEXT, Z)
            issue(1, GRADS_FIRST, GRADS_NEXT)
        if s == min(1, HZ - 2):
            issue(1, GRADS_NEXT, Z)
        if s == back_at:
            backward_start()
    forward_parts(zr)
    back_done = HZ - 2 - back_at

    p1_finish()
    sums = sum_out[...].reshape(TOK, 2 * EL)
    weights_exp = jnp.exp(sums[:, 0:E])
    prob_ref[...] = weights_exp / jnp.sum(weights_exp, axis=1, keepdims=True)

    spot = rem(xy, S)
    first_owner = rem(div(xy, S) - z + Z, Z)
    owners = [first_owner + m * Z for m in range(S)]
    pair_row = lax.broadcasted_iota(jnp.int32, (PAIR, 2 * EL), 0)
    pair_lane = lax.broadcasted_iota(jnp.int32, (PAIR, 2 * EL), 1)
    pair_expert = c * 2 + jnp.where(pair_row >= CAP, 1, 0)

    def w_copy(m):
        return remote(
            w_send.at[m], w_in.at[spot], wt_s.at[m], wt_r.at[spot], (dp, owners[m])
        )

    def w_arrival(b):
        return remote(w_send.at[b], w_in.at[b], wt_s.at[b], wt_r.at[b], (dp, zr * S + b))

    for m in range(S):
        spread = dot_nn(place[owners[m], c], prob_ref[...].astype(BF))
        if E < 2 * EL:
            spread = jnp.concatenate([spread, jnp.zeros((PAIR, 2 * EL - E), F32)], axis=1)
        spread = jnp.where(pair_lane == owners[m] * 4 + pair_expert, spread, 0.0)
        column = jnp.sum(spread, axis=1, keepdims=True)
        w_send[m] = jnp.broadcast_to(column, (PAIR, 2 * EL)).astype(BF)

        @pl.when(owners[m] != xy)
        def _(m=m):
            w_copy(m).start()

        @pl.when(owners[m] == xy)
        def _(m=m):
            w_in[spot] = w_send[m]

    for s in range(back_done, HZ - 1):
        backward_parts(*two_places(HZ - 1 - s))
        rs_step(2, s)
        rs_step(3, s)
    backward_parts(zr)

    for b in range(S):

        @pl.when(zr * S + b != xy)
        def _(b=b):
            w_arrival(b).wait_recv()

    def total(k, r, cols):
        own, got = sums_of(k)
        value = own[zr, r, :, cols].astype(F32)
        return (
            value
            + got[0, HZ - 1, r, :, cols].astype(F32)
            + got[1, HZ - 1, r, :, cols].astype(F32)
        )

    dots = []
    for j in range(2):
        rs_end(j)
        rs_end(2 + j)
        weight = jnp.concatenate(
            [w_in[b].astype(F32)[j * CAP : (j + 1) * CAP, 0:1] for b in range(S)], axis=0
        )
        dot = jnp.zeros((SC, 1), F32)
        for r in range(2):
            raw = total(2 + j, r, slice(0, HH))
            gate = total(j, r, slice(0, HH))
            up = total(j, r, slice(HH, H))
            sig = 1.0 / (1.0 + jnp.exp(-gate))
            silu = gate * sig
            hidden = silu * up
            d_hidden = raw * weight
            full[j, zr, r, :, 0:HH] = (
                d_hidden * up * sig * (1.0 + gate * (1.0 - sig))
            ).astype(BF)
            full[j, zr, r, :, HH:H] = (d_hidden * silu).astype(BF)
            full_b[j, zr, r] = (hidden * weight).astype(BF)
            dot = dot + jnp.sum(hidden * raw, axis=1, keepdims=True)
        ag_start(j)
        ag_start(2 + j)
        dots.append(dot)

    def dots_copy(b):
        return remote(
            dots_send.at[b], dots_in.at[div(xy, Z)], dt_s.at[b], dt_r.at[div(xy, Z)], (dp, zr * S + b)
        )

    def dots_arrival(m):
        return remote(dots_send.at[m], dots_in.at[m], dt_s.at[m], dt_r.at[m], (dp, owners[m]))

    for b in range(S):
        value = jnp.concatenate(
            [dots[0][b * CAP : (b + 1) * CAP], dots[1][b * CAP : (b + 1) * CAP]], axis=0
        )
        value = jnp.broadcast_to(value, (PAIR, 2 * EL))
        high = value.astype(BF).astype(F32)
        dots_send[b] = jnp.where(pair_lane < EL, high, value - high).astype(BF)

        @pl.when(zr * S + b != xy)
        def _(b=b):
            dots_copy(b).start()

        @pl.when(zr * S + b == xy)
        def _(b=b):
            dots_in[div(xy, Z)] = dots_send[b]

    def back_copy(source, core):
        q2 = source * CORES + core
        return remote(
            back_send.at[source, core], back_in.at[q],
            bk_s.at[q2], bk_r.at[q], in_plane(source, core),
        )

    def back_arrival(owner, core):
        q2 = owner * CORES + core
        return remote(
            back_send.at[owner, core], back_in.at[q2],
            bk_s.at[q2], bk_r.at[q2], in_plane(owner, core),
        )

    def send_back(*places):
        values = []
        for j in range(2):
            value = None
            for r in range(2):
                cols = slice(r * HH, (r + 1) * HH)
                both = jnp.concatenate([full[j, t, r] for t in places], axis=0)
                term = dot_nt(both[:, 0:HH], wg[j, :, cols]) + dot_nt(
                    both[:, HH:H], wu[j, :, cols]
                )
                value = term if value is None else value + term
            values.append(value)
        for i, t in enumerate(places):
            for b in range(S):
                at = slice(i * SC + b * CAP, i * SC + (b + 1) * CAP)
                block = jnp.concatenate([values[0][at], values[1][at]], axis=0).astype(BF)
                source = t * S + b
                for h in range(CORES):
                    back_send[source, h] = block[:, h * W : (h + 1) * W]
                for core in cores:
                    if core is other:
                        back_copy(source, core).start()
                    else:

                        @pl.when(source != xy)
                        def _(source=source):
                            back_copy(source, c).start()

                        @pl.when(source == xy)
                        def _(source=source):
                            back_in[q] = back_send[source, c]

    def top_copy(j):
        return remote(
            top_in.at[first_owner, c], top_in.at[first_owner, c], tp_s.at[j], tp_r.at[dp], (j, xy)
        )

    def top_arrival(j):
        w = rem(div(xy, S) - div(j, CORES) + Z, Z)
        ref = top_in.at[w, rem(j, CORES)]
        return remote(ref, ref, tp_s.at[j], tp_r.at[j], (j, xy))

    def send_dots():
        for m in range(S):

            @pl.when(owners[m] != xy)
            def _(m=m):
                dots_arrival(m).wait_recv()

        top = None
        for m in range(S):
            row = 2 * m + jnp.where(pair_row >= CAP, 1, 0)
            lanes = jnp.where(pair_lane >= EL, pair_lane - EL + 4, pair_lane)
            keep = (lanes == jnp.where(pair_lane >= EL, row + 4, row))
            masked = jnp.where(keep, dots_in[m].astype(F32), 0.0).astype(BF)
            term = dot_tn(masked, place[owners[m], c])
            top = term if top is None else top + term
        top_in[first_owner, c] = jnp.concatenate([top[0:4], top[EL : EL + 4]], axis=0)
        loop(1, ND, lambda k: top_copy(rem(dp + k, ND)).start())

    def router_gradients():
        loop(1, ND, lambda k: top_arrival(rem(dp + k, ND)).wait_recv())
        count = Z * CORES * 8
        at = lax.broadcasted_iota(jnp.int32, (count, E), 0)
        expert = lax.broadcasted_iota(jnp.int32, (count, E), 1)
        group, core, sub = div(at, 8 * CORES), rem(div(at, 8), CORES), rem(at, 4)
        named = (group + div(sub, 2) * Z) * 4 + core * 2 + rem(sub, 2)
        pick = jnp.where((named == expert), 1.0, 0.0).astype(BF)
        top = dot_tn(top_in[...].reshape(count, TOK).astype(BF), pick)
        mean = sum_out[...].reshape(TOK, 2 * EL)[:, EL : EL + E]
        d_prob = jnp.where(chosen_ref[...] > 0.5, top, mean)
        prob = prob_ref[...]
        dlogits = prob * (d_prob - jnp.sum(prob * d_prob, axis=1, keepdims=True))
        high, low = split_two(dlogits)
        dlog_hi[...] = high
        dlog_lo[...] = low
        router_part = dot_tn(high, tokens[...]) + dot_tn(low, tokens[...])
        blocks = jnp.concatenate(
            [router_part[:, h * 128 : (h + 1) * 128] for h in range(W // 128)], axis=0
        )
        gr_src[...] = blocks.reshape(side, E * W // (128 * side), 128)
        p2_send()

    actions = [send_dots, router_gradients, p2_middle, p2_reduce]
    send_back(zr)
    for s in range(HZ):
        ag_step(0, s)
        ag_step(2, s)
        ag_step(1, s)
        send_back(*(two_places(1 + s) if s < HZ - 1 else (rem(zr + HZ, Z),)))
        ag_step(3, s)
        for action in actions[s : s + 1] if s < HZ - 1 else actions[s:]:
            action()

    def give(i, j):
        out = (grad_gate, grad_up, grad_down)[i]
        buf = (out_gate, out_up, out_down)[i]
        return remote(
            buf.at[j], out.at[c * 2 + j], ox_s.at[i, j], ox_r.at[i, j], twin
        )

    def take(i, j):
        out = (grad_gate, grad_up, grad_down)[i]
        buf = (out_gate, out_up, out_down)[i]
        return remote(
            buf.at[j], out.at[other * 2 + j], ox_s.at[i, j], ox_r.at[i, j], twin
        )

    for mine_now in (False, True):
        features = half if mine_now else other_half
        for j in range(2):
            some = rows[0, j, :, features]
            for r in range(2):
                cols = slice(r * HH, (r + 1) * HH)
                both = full[j, :, r].reshape(ROWS, H)
                gate = dot_tn(some, both[:, 0:HH]).astype(BF)
                up = dot_tn(some, both[:, HH:H]).astype(BF)
                if mine_now:
                    grad_gate[c * 2 + j, :, cols] = gate
                    grad_up[c * 2 + j, :, cols] = up
                else:
                    out_gate[j, :, cols] = gate
                    out_up[j, :, cols] = up
            if not mine_now:
                give(0, j).start()
                give(1, j).start()
        for j in range(2):
            some = rows[1, j, :, features]
            for r in range(2):
                units = slice(r * HH, (r + 1) * HH)
                hid = full_b[j, :, r].reshape(ROWS, HH)
                down = dot_tn(hid, some).astype(BF)
                if mine_now:
                    grad_down[c * 2 + j, units, :] = down
                else:
                    out_down[j, units, :] = down
            if not mine_now:
                give(2, j).start()

    def other_devices(action):
        action(xy, other)

        def body(k):
            owner = rem(xy + k, NE)
            for core in range(CORES):
                action(owner, core)

        loop(1, NE, body)

    other_devices(lambda o, h: back_arrival(o, h).wait_recv())
    router_term = dot_nn(dlog_hi[...], w_router[...]) + dot_nn(dlog_lo[...], w_router[...])
    token_term = dot_tn(
        place[...].reshape(E * CAP, TOK), back_in[...].reshape(E * CAP, W)
    )
    grad_tokens[...] = (token_term + router_term).astype(BF)
    p2_finish()
    blocks = gr_out[...].reshape(W // 128, E, 128)
    for h in range(W // 128):
        grad_router[:, h * 128 : (h + 1) * 128] = blocks[h]

    def sent(owner, core):
        rows_copy(0, owner, core).wait_send()
        rows_copy(1, owner, core).wait_send()
        back_copy(owner, core).wait_send()

    other_devices(sent)
    for copy in weight_copies:
        copy.wait_send()
    p1_drain()
    p2_drain()
    loop(1, ND, lambda k: top_copy(rem(dp + k, ND)).wait_send())

    for k in range(4):
        for r in range(2):
            for s in range(HZ):
                rs_copy(k, r, s).wait_send()
                ag_copy(k, r, s).wait_send()

    for m in range(S):

        @pl.when(owners[m] != xy)
        def _(m=m):
            w_copy(m).wait_send()

    for b in range(S):

        @pl.when(zr * S + b != xy)
        def _(b=b):
            dots_copy(b).wait_send()

    for i in range(3):
        for j in range(2):
            give(i, j).wait_send()
            take(i, j).wait_recv()


def per_device(tokens, cotangent, routing, w_router, running_mean, w_gate, w_up, w_down):
    NE = lax.axis_size("expert")
    ND = lax.axis_size("dp")
    Z = ND // CORES
    local_count, W, H = w_gate.shape
    E = NE * local_count
    TOK, top = routing.shape
    routing, w_router = routing.T, w_router.T
    CAP = 3 * TOK * top // (2 * E)
    NQ = NE * CORES
    S = NE // Z
    HZ = Z // 2
    PAIR, ROWS = 2 * CAP, NE * CAP
    side = 4 if NE % 4 == 0 else NE
    GR = E * W // (128 * side)
    sizes = (NE, Z, E, TOK, H, W, CAP)
    vmem = pl.BlockSpec(memory_space=pltpu.VMEM)
    hbm = pl.BlockSpec(memory_space=pl.ANY)
    dma = pltpu.SemaphoreType.DMA
    scratch = [
        pltpu.VMEM((NE, CORES, PAIR, TOK), BF),
        pltpu.VMEM((2, NQ, PAIR, W), BF),
        pltpu.VMEM((2, CORES, NE, PAIR, W), BF),
        pltpu.VMEM((2, 2, ROWS, 2 * W), BF),
        pltpu.VMEM((2, 2 * W, H), BF),
        pltpu.VMEM((2, 2 * W, H), BF),
        pltpu.VMEM((2, 2, H, W), BF),
        pltpu.VMEM((2, Z, 2, S * CAP, H), BF),
        pltpu.VMEM((2, 2, HZ, 2, S * CAP, H), BF),
        pltpu.VMEM((2, Z, 2, S * CAP, H), BF),
        pltpu.VMEM((2, Z, 2, S * CAP, H // 2), BF),
        pltpu.VMEM((2, 2, HZ, 2, S * CAP, H // 2), BF),
        pltpu.VMEM((2, Z, 2, S * CAP, H // 2), BF),
        pltpu.VMEM((ND, TOK // ND, 128), F32),
        pltpu.VMEM((ND, TOK // ND, 128), F32),
        pltpu.VMEM((ND, TOK // ND, 128), F32),
        pltpu.VMEM((side, GR, 128), F32),
        pltpu.VMEM((side, GR, 128), F32),
        pltpu.VMEM((NE // side, GR, 128), F32),
        pltpu.VMEM((side, GR, 128), F32),
        pltpu.VMEM((Z, CORES, 8, TOK), F32),
        pltpu.VMEM((TOK, E), F32),
        pltpu.VMEM((TOK, E), F32),
        pltpu.VMEM((S, PAIR, 128), BF),
        pltpu.VMEM((S, PAIR, 128), BF),
        pltpu.VMEM((S, PAIR, 128), BF),
        pltpu.VMEM((S, PAIR, 128), BF),
        pltpu.VMEM((TOK, E), BF),
        pltpu.VMEM((TOK, E), BF),
        pltpu.VMEM((NE, CORES, PAIR, W), BF),
        pltpu.VMEM((NQ, PAIR, W), BF),
        pltpu.VMEM((2, W, H), BF),
        pltpu.VMEM((2, W, H), BF),
        pltpu.VMEM((2, H, W), BF),
        dma((2, NQ)), dma((2, NQ)),
        dma((3,)), dma((3,)), dma((3,)),
        dma((2, ND)), dma((2, ND)),
        dma((3, NE)), dma((3, NE)),
        dma((ND,)), dma((ND,)),
        dma((4, 2, HZ)), dma((4, 2, HZ)),
        dma((4, 2, HZ)), dma((4, 2, HZ)),
        dma((S,)), dma((S,)),
        dma((S,)), dma((S,)),
        dma((NQ,)), dma((NQ,)),
        dma((3, 2)), dma((3, 2)),
    ]
    results = pl.pallas_call(
        functools.partial(kernel, sizes),
        out_shape=(
            pltpu.VMEM((TOK, W), BF),
            pltpu.VMEM((E, W), F32),
            pltpu.VMEM((local_count, W, H), BF),
            pltpu.VMEM((local_count, W, H), BF),
            pltpu.VMEM((local_count, H, W), BF),
        ),
        in_specs=[vmem] * 5 + [hbm] * 3,
        out_specs=(vmem, vmem, vmem, vmem, vmem),
        scratch_shapes=scratch,
        compiler_params=pltpu.CompilerParams(
            collective_id=0, has_side_effects=True, vmem_limit_bytes=56 * 1024 * 1024
        ),
        cost_estimate=pl.CostEstimate(
            flops=6 * 10**9, bytes_accessed=10**7, transcendentals=10**5
        ),
    )(tokens, cotangent, routing, w_router, running_mean, w_gate, w_up, w_down)
    grad_tokens, grad_router, *rest = results
    return (grad_tokens, grad_router.T, *rest)


def solution(mesh):
    return jax.shard_map(
        per_device,
        mesh=mesh,
        in_specs=(
            P("expert", "dp"),
            P("expert", "dp"),
            P("expert", None),
            P("dp", None),
            P(None, "dp"),
            P("expert", "dp", None),
            P("expert", "dp", None),
            P("expert", None, "dp"),
        ),
        out_specs=(
            P("expert", "dp"),
            P("dp", None),
            P("expert", "dp", None),
            P("expert", "dp", None),
            P("expert", None, "dp"),
        ),
        check_vma=False,
    )
```

```python
import functools

import jax
import jax.numpy as jnp
from jax import lax
from jax.experimental import pallas as pl
from jax.experimental.pallas import tpu as pltpu
from jax.sharding import PartitionSpec as P

MESH = pl.DeviceIdType.MESH
BF = jnp.bfloat16
F32 = jnp.float32
CORES = 2
ROWS_FIRST = 3
ROWS_NEXT = 8
GRADS_FIRST = 1
GRADS_NEXT = 4
BACK_AT = 0


def rem(a, n):
    return lax.rem(a, jnp.int32(n))


def div(a, n):
    return lax.div(a, jnp.int32(n))


def remote(src, dst, send_sem, recv_sem, device):
    return pltpu.make_async_remote_copy(
        src_ref=src,
        dst_ref=dst,
        send_sem=send_sem,
        recv_sem=recv_sem,
        device_id=device,
        device_id_type=MESH,
    )


def loop(lower, upper, body):
    def step(i, carry):
        body(i)
        return carry

    lax.fori_loop(lower, upper, step, 0)


def dot_nn(a, b):
    return jnp.dot(a, b, preferred_element_type=F32)


def dot_nt(a, b):
    return lax.dot_general(a, b, (((1,), (1,)), ((), ())), preferred_element_type=F32)


def dot_tn(a, b):
    return lax.dot_general(a, b, (((0,), (0,)), ((), ())), preferred_element_type=F32)


def split_two(value):
    high = value.astype(BF)
    low = (value - high.astype(F32)).astype(BF)
    return high, low


def kernel(
    sizes,
    tokens, cotangent, routing, w_router, running_mean, w_gate, w_up, w_down,
    grad_tokens, grad_router, grad_gate, grad_up, grad_down,
    place, send_rows, in_rows, rows, wg, wu, wd,
    part, recv, full, part_b, recv_b, full_b,
    sum_src, sum_in, sum_out, gr_src, gx_in, gy_in, gr_out, top_in,
    prob_ref, chosen_ref, w_send, w_in, dots_send, dots_in, dlog_hi, dlog_lo,
    back_send, back_in, out_gate, out_up, out_down,
    rows_s, rows_r, wx_s, wx_r, wl_s,
    p1_s, p1_r, p2_s, p2_r, tp_s, tp_r,
    rs_s, rs_r, ag_s, ag_r,
    wt_s, wt_r, dt_s, dt_r, bk_s, bk_r,
    ox_s, ox_r,
):
    NE, Z, E, TOK, H, W, CAP = sizes
    ND = Z * CORES
    NQ = NE * CORES
    S = NE // Z
    HZ = Z // 2
    HH = H // 2
    SC = S * CAP
    EL = 64
    PAIR = 2 * CAP
    ROWS = NE * CAP

    dp = lax.axis_index("dp")
    xy = lax.axis_index("expert")
    z = div(dp, CORES)
    c = rem(dp, CORES)
    other = 1 - c
    q = xy * CORES + c
    zr = rem(z + xy, Z)
    right = rem(z + 1, Z)
    left = rem(z + Z - 1, Z)
    twin = (z * CORES + other, xy)

    def in_plane(owner, core):
        return (z * CORES + core, owner)

    cores = (c, other)

    def each_target(i, action):
        distance = HZ + div(i + 1, 2) * (1 - 2 * rem(i, 2))
        first = rem(div(xy, S) - z - distance + 2 * Z, Z)
        for m in range(S):
            owner = first + m * Z
            for core in cores:
                if core is c:
                    pl.when(owner != xy)(lambda owner=owner, core=core: action(owner, core))
                else:
                    action(owner, core)

    def issue(which, first, last):
        loop(
            first,
            last,
            lambda i: each_target(i, lambda o, h: rows_copy(which, o, h).start()),
        )

    def each_source(t, action):
        for b in range(S):
            source = t * S + b
            for core in cores:
                if core is c:
                    pl.when(source != xy)(lambda source=source, core=core: action(source, core))
                else:
                    action(source, core)

    barrier = pltpu.get_barrier_semaphore()

    def greet(*device):
        pl.semaphore_signal(barrier, inc=1, device_id=device, device_id_type=MESH)

    def greet_plane(k):
        for core in range(CORES):
            greet(z * CORES + core, rem(xy + k, NE))

    def greet_column(k):
        for core in range(CORES):
            greet(rem(z + k, Z) * CORES + core, xy)

    greet(*twin)
    loop(1, NE, greet_plane)
    loop(1, Z, greet_column)

    def own_weights(i, src, dst):
        return pltpu.make_async_copy(src, dst, wl_s.at[i])

    half = pl.ds(pl.multiple_of(c * W, W), W)
    mine = pl.ds(c * 2, 2)
    theirs = pl.ds(other * 2, 2)
    own_copies = [
        own_weights(0, w_gate.at[mine], wg.at[:, half, :]),
        own_weights(1, w_up.at[mine], wu.at[:, half, :]),
        own_weights(2, w_down.at[mine], wd.at[c]),
    ]
    for copy in own_copies:
        copy.start()

    route = routing[...]
    row_e = lax.broadcasted_iota(jnp.int32, (E, TOK), 0)
    has = jnp.zeros((E, TOK), F32)
    for k in range(route.shape[0]):
        has = has + jnp.where(route[k : k + 1, :] == row_e, 1.0, 0.0)
    t_row = lax.broadcasted_iota(jnp.int32, (TOK, TOK), 0)
    t_col = lax.broadcasted_iota(jnp.int32, (TOK, TOK), 1)
    before = jnp.where(t_row < t_col, 1.0, 0.0).astype(BF)
    same = jnp.where(t_row == t_col, 1.0, 0.0).astype(BF)
    pos = jnp.where(has > 0.5, dot_nn(has.astype(BF), before), -1.0)
    chosen_ref[...] = dot_nt(same, has.astype(BF))
    slot_iota = lax.broadcasted_iota(jnp.int32, (E, CAP, TOK), 1).astype(F32)
    placing = jnp.where(pos[:, None, :] == slot_iota, 1.0, 0.0)
    placing = placing.reshape(E * CAP, TOK).astype(BF)
    place[...] = placing.reshape(NE, CORES, PAIR, TOK)
    send_rows[0] = dot_nn(placing, tokens[...]).astype(BF).reshape(NQ, PAIR, W)
    send_rows[1] = dot_nn(placing, cotangent[...]).astype(BF).reshape(NQ, PAIR, W)

    pl.semaphore_wait(barrier, NQ - 1 + CORES * (Z - 1))

    def rows_copy(which, owner, core):
        q2 = owner * CORES + core
        return remote(
            send_rows.at[which, q2], in_rows.at[which, c, xy],
            rows_s.at[which, q2], rows_r.at[which, q], in_plane(owner, core),
        )

    def rows_arrival(which, source, core):
        q2 = source * CORES + core
        return remote(
            send_rows.at[which, q2], in_rows.at[which, core, source],
            rows_s.at[which, q2], rows_r.at[which, q2], in_plane(source, core),
        )

    weight_copies = [
        remote(w_gate.at[theirs], wg.at[:, half, :], wx_s.at[0], wx_r.at[0], twin),
        remote(w_up.at[theirs], wu.at[:, half, :], wx_s.at[1], wx_r.at[1], twin),
        remote(w_down.at[theirs], wd.at[c], wx_s.at[2], wx_r.at[2], twin),
    ]
    other_half = pl.ds(pl.multiple_of(other * W, W), W)
    weight_arrivals = [
        remote(w_gate.at[theirs], wg.at[:, other_half, :], wx_s.at[0], wx_r.at[0], twin),
        remote(w_up.at[theirs], wu.at[:, other_half, :], wx_s.at[1], wx_r.at[1], twin),
        remote(w_down.at[theirs], wd.at[other], wx_s.at[2], wx_r.at[2], twin),
    ]
    weight_copies[0].start()
    weight_copies[1].start()
    issue(0, 0, ROWS_FIRST)
    in_rows[0, c, xy] = send_rows[0, q]
    in_rows[1, c, xy] = send_rows[1, q]

    def sum_blocks(n, index, peer, src, into, out, sem_s, sem_r):
        def scatter(j):
            return remote(src.at[j], into.at[index], sem_s.at[0, j], sem_r.at[0, index], peer(j))

        def scatter_arrival(j):
            return remote(src.at[j], into.at[j], sem_s.at[0, j], sem_r.at[0, j], peer(j))

        def gather(j):
            return remote(
                out.at[index], out.at[index], sem_s.at[1, j], sem_r.at[1, index], peer(j)
            )

        def gather_arrival(j):
            return remote(out.at[j], out.at[j], sem_s.at[1, j], sem_r.at[1, j], peer(j))

        def send():
            loop(1, n, lambda k: scatter(rem(index + k, n)).start())
            into[index] = src[index]

        def reduce():
            loop(1, n, lambda k: scatter_arrival(rem(index + k, n)).wait_recv())
            out[index] = jnp.sum(into[...], axis=0)
            loop(1, n, lambda k: gather(rem(index + k, n)).start())

        def finish():
            loop(1, n, lambda k: gather_arrival(rem(index + k, n)).wait_recv())

        def drain():
            loop(1, n, lambda k: scatter(rem(index + k, n)).wait_send())
            loop(1, n, lambda k: gather(rem(index + k, n)).wait_send())

        return send, reduce, finish, drain

    p1_send, p1_reduce, p1_finish, p1_drain = sum_blocks(
        ND, dp, lambda j: (j, xy), sum_src, sum_in, sum_out, p1_s, p1_r
    )
    side = 4 if NE % 4 == 0 else NE
    x, y, NY = rem(xy, side), div(xy, side), NE // side

    def gx_copy(j):
        return remote(
            gr_src.at[j], gx_in.at[x], p2_s.at[0, j], p2_r.at[0, x], (dp, y * side + j)
        )

    def gx_arrival(j):
        return remote(
            gr_src.at[j], gx_in.at[j], p2_s.at[0, j], p2_r.at[0, j], (dp, y * side + j)
        )

    def gy_copy(j):
        return remote(
            gy_in.at[y], gy_in.at[y], p2_s.at[1, j], p2_r.at[1, y], (dp, j * side + x)
        )

    def gy_arrival(j):
        return remote(
            gy_in.at[j], gy_in.at[j], p2_s.at[1, j], p2_r.at[1, j], (dp, j * side + x)
        )

    def gz_copy(j):
        return remote(
            gr_out.at[x], gr_out.at[x], p2_s.at[2, j], p2_r.at[2, x], (dp, y * side + j)
        )

    def gz_arrival(j):
        return remote(
            gr_out.at[j], gr_out.at[j], p2_s.at[2, j], p2_r.at[2, j], (dp, y * side + j)
        )

    def p2_send():
        for k in range(1, side):
            gx_copy(rem(x + k, side)).start()
        gx_in[x] = gr_src[x]

    def p2_middle():
        for k in range(1, side):
            gx_arrival(rem(x + k, side)).wait_recv()
        gy_in[y] = jnp.sum(gx_in[...], axis=0)
        for k in range(1, NY):
            gy_copy(rem(y + k, NY)).start()

    def p2_reduce():
        for k in range(1, NY):
            gy_arrival(rem(y + k, NY)).wait_recv()
        gr_out[x] = jnp.sum(gy_in[...], axis=0)
        for k in range(1, side):
            gz_copy(rem(x + k, side)).start()

    def p2_finish():
        for k in range(1, side):
            gz_arrival(rem(x + k, side)).wait_recv()

    def p2_drain():
        for k in range(1, side):
            gx_copy(rem(x + k, side)).wait_send()
            gz_copy(rem(x + k, side)).wait_send()
        for k in range(1, NY):
            gy_copy(rem(y + k, NY)).wait_send()

    def packed(first, second, count):
        if E < EL:
            gap = jnp.zeros((TOK, EL - E), F32)
            first = jnp.concatenate([first, gap], axis=1)
            second = jnp.concatenate([second, gap], axis=1)
        return jnp.concatenate([first, second], axis=1).reshape(count, TOK // count, 2 * EL)

    logits_part = dot_nt(tokens[...], w_router[...])
    mean_part = dot_nt(cotangent[...], running_mean[...])
    sum_src[...] = packed(logits_part, mean_part, ND)
    p1_send()

    def order_rows(which, t):
        each_source(t, lambda o, h: rows_arrival(which, o, h).wait_recv())
        at = pl.ds(pl.multiple_of(t * SC, SC), SC)
        for h in range(CORES):
            block = in_rows[which, h, pl.ds(t * S, S)].astype(F32)
            for j in range(2):
                piece = block[:, j * CAP : (j + 1) * CAP, :].reshape(SC, W)
                rows[which, j, at, h * W : (h + 1) * W] = piece.astype(BF)

    def some_rows(which, j, places):
        return jnp.concatenate(
            [rows[which, j, pl.ds(pl.multiple_of(t * SC, SC), SC), :] for t in places], axis=0
        )

    def forward_parts(*places, ordered=False):
        for t in places:
            if not ordered:
                order_rows(0, t)
        for j in range(2):
            some = some_rows(0, j, places)
            for r in range(2):
                cols = slice(r * HH, (r + 1) * HH)
                gate = dot_nn(some, wg[j, :, cols]).astype(BF)
                up = dot_nn(some, wu[j, :, cols]).astype(BF)
                for i, t in enumerate(places):
                    part[j, t, r, :, 0:HH] = gate[i * SC : (i + 1) * SC]
                    part[j, t, r, :, HH:H] = up[i * SC : (i + 1) * SC]

    def backward_parts(*places):
        for t in places:
            order_rows(1, t)
        for j in range(2):
            some = some_rows(1, j, places)
            for r in range(2):
                units = slice(r * HH, (r + 1) * HH)
                value = dot_nt(some[:, 0:W], wd[0, j, units, :]) + dot_nt(
                    some[:, W : 2 * W], wd[1, j, units, :]
                )
                value = value.astype(BF)
                for i, t in enumerate(places):
                    part_b[j, t, r] = value[i * SC : (i + 1) * SC]

    def ring_peer(r):
        return ((right if r == 0 else left) * CORES + c, xy)

    def sums_of(k):
        return (part.at[k], recv.at[k]) if k < 2 else (part_b.at[k - 2], recv_b.at[k - 2])

    def gathered(k):
        return full.at[k] if k < 2 else full_b.at[k - 2]

    def rs_copy(k, r, s):
        t = rem(zr + HZ - s, Z) if r == 0 else rem(zr - HZ + s + Z, Z)
        own, got = sums_of(k)
        if s == 0:
            src, dst = own.at[t, r], got.at[r, 0, r]
        else:
            src, dst = own.at[t], got.at[r, s]
        return remote(src, dst, rs_s.at[k, r, s], rs_r.at[k, r, s], ring_peer(r))

    def rs_step(k, s):
        own, got = sums_of(k)
        for r in range(2):
            rs_copy(k, r, s).wait_recv()
            t = rem(zr + HZ - s - 1, Z) if r == 0 else rem(zr - HZ + s + 1 + Z, Z)
            if s == 0:
                own[t, r] = (own[t, r].astype(F32) + got[r, 0, r].astype(F32)).astype(BF)
            else:
                own[t] = (own[t].astype(F32) + got[r, s].astype(F32)).astype(BF)
            rs_copy(k, r, s + 1).start()

    def rs_start(k):
        for r in range(2):
            rs_copy(k, r, 0).start()

    def rs_end(k):
        for r in range(2):
            rs_copy(k, r, HZ - 1).wait_recv()

    def ag_copy(k, r, s):
        t = rem(zr - s + Z, Z) if r == 0 else rem(zr + s, Z)
        ref = gathered(k).at[t, r] if s == HZ - 1 else gathered(k).at[t]
        return remote(ref, ref, ag_s.at[k, r, s], ag_r.at[k, r, s], ring_peer(r))

    def ag_arrival(k, r, s):
        t = rem(zr - 1 - s + Z, Z) if r == 0 else rem(zr + 1 + s, Z)
        ref = gathered(k).at[t, r] if s == HZ - 1 else gathered(k).at[t]
        return remote(ref, ref, ag_s.at[k, r, s], ag_r.at[k, r, s], ring_peer(r))

    def ag_step(k, s):
        for r in range(2):
            ag_arrival(k, r, s).wait_recv()
            if s < HZ - 1:
                ag_copy(k, r, s + 1).start()

    def ag_start(k):
        for r in range(2):
            ag_copy(k, r, 0).start()

    def two_places(distance):
        return rem(zr + distance, Z), rem(zr - distance + Z, Z)

    def backward_start():
        own_copies[2].wait()
        weight_arrivals[2].wait_recv()
        backward_parts(rem(zr + HZ, Z))
        rs_start(2)
        rs_start(3)

    own_copies[0].wait()
    own_copies[1].wait()
    weight_arrivals[0].wait_recv()
    weight_arrivals[1].wait_recv()
    order_rows(0, rem(zr + HZ, Z))
    issue(0, ROWS_FIRST, ROWS_NEXT)
    weight_copies[2].start()
    issue(1, 0, GRADS_FIRST)
    forward_parts(rem(zr + HZ, Z), ordered=True)
    rs_start(0)
    forward_parts(*two_places(HZ - 1))
    rs_start(1)
    back_at = min(BACK_AT, HZ - 2)
    for s in range(HZ - 1):
        if s > 0:
            forward_parts(*two_places(HZ - 1 - s))
        rs_step(0, s)
        if s > back_at:
            backward_parts(*two_places(HZ - 1 - (s - back_at - 1)))
            rs_step(2, s - back_at - 1)
            rs_step(3, s - back_at - 1)
        rs_step(1, s)
        if s == 0:
            p1_reduce()
            issue(0, ROWS_NEXT, Z)
            issue(1, GRADS_FIRST, GRADS_NEXT)
        if s == min(1, HZ - 2):
            issue(1, GRADS_NEXT, Z)
        if s == back_at:
            backward_start()
    forward_parts(zr)
    back_done = HZ - 2 - back_at

    p1_finish()
    sums = sum_out[...].reshape(TOK, 2 * EL)
    weights_exp = jnp.exp(sums[:, 0:E])
    prob_ref[...] = weights_exp / jnp.sum(weights_exp, axis=1, keepdims=True)

    spot = rem(xy, S)
    first_owner = rem(div(xy, S) - z + Z, Z)
    owners = [first_owner + m * Z for m in range(S)]
    pair_row = lax.broadcasted_iota(jnp.int32, (PAIR, 2 * EL), 0)
    pair_lane = lax.broadcasted_iota(jnp.int32, (PAIR, 2 * EL), 1)
    pair_expert = c * 2 + jnp.where(pair_row >= CAP, 1, 0)

    def w_copy(m):
        return remote(
            w_send.at[m], w_in.at[spot], wt_s.at[m], wt_r.at[spot], (dp, owners[m])
        )

    def w_arrival(b):
        return remote(w_send.at[b], w_in.at[b], wt_s.at[b], wt_r.at[b], (dp, zr * S + b))

    for m in range(S):
        spread = dot_nn(place[owners[m], c], prob_ref[...].astype(BF))
        if E < 2 * EL:
            spread = jnp.concatenate([spread, jnp.zeros((PAIR, 2 * EL - E), F32)], axis=1)
        spread = jnp.where(pair_lane == owners[m] * 4 + pair_expert, spread, 0.0)
        column = jnp.sum(spread, axis=1, keepdims=True)
        w_send[m] = jnp.broadcast_to(column, (PAIR, 2 * EL)).astype(BF)

        @pl.when(owners[m] != xy)
        def _(m=m):
            w_copy(m).start()

        @pl.when(owners[m] == xy)
        def _(m=m):
            w_in[spot] = w_send[m]

    for s in range(back_done, HZ - 1):
        backward_parts(*two_places(HZ - 1 - s))
        rs_step(2, s)
        rs_step(3, s)
    backward_parts(zr)

    for b in range(S):

        @pl.when(zr * S + b != xy)
        def _(b=b):
            w_arrival(b).wait_recv()

    def total(k, r, cols):
        own, got = sums_of(k)
        value = own[zr, r, :, cols].astype(F32)
        return (
            value
            + got[0, HZ - 1, r, :, cols].astype(F32)
            + got[1, HZ - 1, r, :, cols].astype(F32)
        )

    dots = []
    for j in range(2):
        rs_end(j)
        rs_end(2 + j)
        weight = jnp.concatenate(
            [w_in[b].astype(F32)[j * CAP : (j + 1) * CAP, 0:1] for b in range(S)], axis=0
        )
        dot = jnp.zeros((SC, 1), F32)
        for r in range(2):
            raw = total(2 + j, r, slice(0, HH))
            gate = total(j, r, slice(0, HH))
            up = total(j, r, slice(HH, H))
            sig = 1.0 / (1.0 + jnp.exp(-gate))
            silu = gate * sig
            hidden = silu * up
            d_hidden = raw * weight
            full[j, zr, r, :, 0:HH] = (
                d_hidden * up * sig * (1.0 + gate * (1.0 - sig))
            ).astype(BF)
            full[j, zr, r, :, HH:H] = (d_hidden * silu).astype(BF)
            full_b[j, zr, r] = (hidden * weight).astype(BF)
            dot = dot + jnp.sum(hidden * raw, axis=1, keepdims=True)
        ag_start(j)
        ag_start(2 + j)
        dots.append(dot)

    def dots_copy(b):
        return remote(
            dots_send.at[b], dots_in.at[div(xy, Z)], dt_s.at[b], dt_r.at[div(xy, Z)], (dp, zr * S + b)
        )

    def dots_arrival(m):
        return remote(dots_send.at[m], dots_in.at[m], dt_s.at[m], dt_r.at[m], (dp, owners[m]))

    for b in range(S):
        value = jnp.concatenate(
            [dots[0][b * CAP : (b + 1) * CAP], dots[1][b * CAP : (b + 1) * CAP]], axis=0
        )
        value = jnp.broadcast_to(value, (PAIR, 2 * EL))
        high = value.astype(BF).astype(F32)
        dots_send[b] = jnp.where(pair_lane < EL, high, value - high).astype(BF)

        @pl.when(zr * S + b != xy)
        def _(b=b):
            dots_copy(b).start()

        @pl.when(zr * S + b == xy)
        def _(b=b):
            dots_in[div(xy, Z)] = dots_send[b]

    def back_copy(source, core):
        q2 = source * CORES + core
        return remote(
            back_send.at[source, core], back_in.at[q],
            bk_s.at[q2], bk_r.at[q], in_plane(source, core),
        )

    def back_arrival(owner, core):
        q2 = owner * CORES + core
        return remote(
            back_send.at[owner, core], back_in.at[q2],
            bk_s.at[q2], bk_r.at[q2], in_plane(owner, core),
        )

    def send_back(*places):
        values = []
        for j in range(2):
            value = None
            for r in range(2):
                cols = slice(r * HH, (r + 1) * HH)
                both = jnp.concatenate([full[j, t, r] for t in places], axis=0)
                term = dot_nt(both[:, 0:HH], wg[j, :, cols]) + dot_nt(
                    both[:, HH:H], wu[j, :, cols]
                )
                value = term if value is None else value + term
            values.append(value)
        for i, t in enumerate(places):
            for b in range(S):
                at = slice(i * SC + b * CAP, i * SC + (b + 1) * CAP)
                block = jnp.concatenate([values[0][at], values[1][at]], axis=0).astype(BF)
                source = t * S + b
                for h in range(CORES):
                    back_send[source, h] = block[:, h * W : (h + 1) * W]
                for core in cores:
                    if core is other:
                        back_copy(source, core).start()
                    else:

                        @pl.when(source != xy)
                        def _(source=source):
                            back_copy(source, c).start()

                        @pl.when(source == xy)
                        def _(source=source):
                            back_in[q] = back_send[source, c]

    def top_copy(j):
        return remote(
            top_in.at[first_owner, c], top_in.at[first_owner, c], tp_s.at[j], tp_r.at[dp], (j, xy)
        )

    def top_arrival(j):
        w = rem(div(xy, S) - div(j, CORES) + Z, Z)
        ref = top_in.at[w, rem(j, CORES)]
        return remote(ref, ref, tp_s.at[j], tp_r.at[j], (j, xy))

    def send_dots():
        for m in range(S):

            @pl.when(owners[m] != xy)
            def _(m=m):
                dots_arrival(m).wait_recv()

        top = None
        for m in range(S):
            row = 2 * m + jnp.where(pair_row >= CAP, 1, 0)
            lanes = jnp.where(pair_lane >= EL, pair_lane - EL + 4, pair_lane)
            keep = (lanes == jnp.where(pair_lane >= EL, row + 4, row))
            masked = jnp.where(keep, dots_in[m].astype(F32), 0.0).astype(BF)
            term = dot_tn(masked, place[owners[m], c])
            top = term if top is None else top + term
        top_in[first_owner, c] = jnp.concatenate([top[0:4], top[EL : EL + 4]], axis=0)
        loop(1, ND, lambda k: top_copy(rem(dp + k, ND)).start())

    def router_gradients():
        loop(1, ND, lambda k: top_arrival(rem(dp + k, ND)).wait_recv())
        count = Z * CORES * 8
        at = lax.broadcasted_iota(jnp.int32, (count, E), 0)
        expert = lax.broadcasted_iota(jnp.int32, (count, E), 1)
        group, core, sub = div(at, 8 * CORES), rem(div(at, 8), CORES), rem(at, 4)
        named = (group + div(sub, 2) * Z) * 4 + core * 2 + rem(sub, 2)
        pick = jnp.where((named == expert), 1.0, 0.0).astype(BF)
        top = dot_tn(top_in[...].reshape(count, TOK).astype(BF), pick)
        mean = sum_out[...].reshape(TOK, 2 * EL)[:, EL : EL + E]
        d_prob = jnp.where(chosen_ref[...] > 0.5, top, mean)
        prob = prob_ref[...]
        dlogits = prob * (d_prob - jnp.sum(prob * d_prob, axis=1, keepdims=True))
        high, low = split_two(dlogits)
        dlog_hi[...] = high
        dlog_lo[...] = low
        router_part = dot_tn(high, tokens[...]) + dot_tn(low, tokens[...])
        blocks = jnp.concatenate(
            [router_part[:, h * 128 : (h + 1) * 128] for h in range(W // 128)], axis=0
        )
        gr_src[...] = blocks.reshape(side, E * W // (128 * side), 128)
        p2_send()

    actions = [send_dots, router_gradients, p2_middle, p2_reduce]
    send_back(zr)
    for s in range(HZ):
        ag_step(0, s)
        ag_step(1, s)
        send_back(*(two_places(1 + s) if s < HZ - 1 else (rem(zr + HZ, Z),)))
        ag_step(2, s)
        ag_step(3, s)
        for action in actions[s : s + 1] if s < HZ - 1 else actions[s:]:
            action()

    def give(i, j):
        out = (grad_gate, grad_up, grad_down)[i]
        buf = (out_gate, out_up, out_down)[i]
        return remote(
            buf.at[j], out.at[c * 2 + j], ox_s.at[i, j], ox_r.at[i, j], twin
        )

    def take(i, j):
        out = (grad_gate, grad_up, grad_down)[i]
        buf = (out_gate, out_up, out_down)[i]
        return remote(
            buf.at[j], out.at[other * 2 + j], ox_s.at[i, j], ox_r.at[i, j], twin
        )

    for mine_now in (False, True):
        features = half if mine_now else other_half
        for j in range(2):
            some = rows[0, j, :, features]
            for r in range(2):
                cols = slice(r * HH, (r + 1) * HH)
                both = full[j, :, r].reshape(ROWS, H)
                gate = dot_tn(some, both[:, 0:HH]).astype(BF)
                up = dot_tn(some, both[:, HH:H]).astype(BF)
                if mine_now:
                    grad_gate[c * 2 + j, :, cols] = gate
                    grad_up[c * 2 + j, :, cols] = up
                else:
                    out_gate[j, :, cols] = gate
                    out_up[j, :, cols] = up
            if not mine_now:
                give(0, j).start()
                give(1, j).start()
        for j in range(2):
            some = rows[1, j, :, features]
            for r in range(2):
                units = slice(r * HH, (r + 1) * HH)
                hid = full_b[j, :, r].reshape(ROWS, HH)
                down = dot_tn(hid, some).astype(BF)
                if mine_now:
                    grad_down[c * 2 + j, units, :] = down
                else:
                    out_down[j, units, :] = down
            if not mine_now:
                give(2, j).start()

    def other_devices(action):
        action(xy, other)

        def body(k):
            owner = rem(xy + k, NE)
            for core in range(CORES):
                action(owner, core)

        loop(1, NE, body)

    other_devices(lambda o, h: back_arrival(o, h).wait_recv())
    router_term = dot_nn(dlog_hi[...], w_router[...]) + dot_nn(dlog_lo[...], w_router[...])
    token_term = dot_tn(
        place[...].reshape(E * CAP, TOK), back_in[...].reshape(E * CAP, W)
    )
    grad_tokens[...] = (token_term + router_term).astype(BF)
    p2_finish()
    blocks = gr_out[...].reshape(W // 128, E, 128)
    for h in range(W // 128):
        grad_router[:, h * 128 : (h + 1) * 128] = blocks[h]

    def sent(owner, core):
        rows_copy(0, owner, core).wait_send()
        rows_copy(1, owner, core).wait_send()
        back_copy(owner, core).wait_send()

    other_devices(sent)
    for copy in weight_copies:
        copy.wait_send()
    p1_drain()
    p2_drain()
    loop(1, ND, lambda k: top_copy(rem(dp + k, ND)).wait_send())

    for k in range(4):
        for r in range(2):
            for s in range(HZ):
                rs_copy(k, r, s).wait_send()
                ag_copy(k, r, s).wait_send()

    for m in range(S):

        @pl.when(owners[m] != xy)
        def _(m=m):
            w_copy(m).wait_send()

    for b in range(S):

        @pl.when(zr * S + b != xy)
        def _(b=b):
            dots_copy(b).wait_send()

    for i in range(3):
        for j in range(2):
            give(i, j).wait_send()
            take(i, j).wait_recv()


def per_device(tokens, cotangent, routing, w_router, running_mean, w_gate, w_up, w_down):
    NE = lax.axis_size("expert")
    ND = lax.axis_size("dp")
    Z = ND // CORES
    local_count, W, H = w_gate.shape
    E = NE * local_count
    TOK, top = routing.shape
    routing, w_router = routing.T, w_router.T
    CAP = 3 * TOK * top // (2 * E)
    NQ = NE * CORES
    S = NE // Z
    HZ = Z // 2
    PAIR, ROWS = 2 * CAP, NE * CAP
    side = 4 if NE % 4 == 0 else NE
    GR = E * W // (128 * side)
    sizes = (NE, Z, E, TOK, H, W, CAP)
    vmem = pl.BlockSpec(memory_space=pltpu.VMEM)
    hbm = pl.BlockSpec(memory_space=pl.ANY)
    dma = pltpu.SemaphoreType.DMA
    scratch = [
        pltpu.VMEM((NE, CORES, PAIR, TOK), BF),
        pltpu.VMEM((2, NQ, PAIR, W), BF),
        pltpu.VMEM((2, CORES, NE, PAIR, W), BF),
        pltpu.VMEM((2, 2, ROWS, 2 * W), BF),
        pltpu.VMEM((2, 2 * W, H), BF),
        pltpu.VMEM((2, 2 * W, H), BF),
        pltpu.VMEM((2, 2, H, W), BF),
        pltpu.VMEM((2, Z, 2, S * CAP, H), BF),
        pltpu.VMEM((2, 2, HZ, 2, S * CAP, H), BF),
        pltpu.VMEM((2, Z, 2, S * CAP, H), BF),
        pltpu.VMEM((2, Z, 2, S * CAP, H // 2), BF),
        pltpu.VMEM((2, 2, HZ, 2, S * CAP, H // 2), BF),
        pltpu.VMEM((2, Z, 2, S * CAP, H // 2), BF),
        pltpu.VMEM((ND, TOK // ND, 128), F32),
        pltpu.VMEM((ND, TOK // ND, 128), F32),
        pltpu.VMEM((ND, TOK // ND, 128), F32),
        pltpu.VMEM((side, GR, 128), F32),
        pltpu.VMEM((side, GR, 128), F32),
        pltpu.VMEM((NE // side, GR, 128), F32),
        pltpu.VMEM((side, GR, 128), F32),
        pltpu.VMEM((Z, CORES, 8, TOK), F32),
        pltpu.VMEM((TOK, E), F32),
        pltpu.VMEM((TOK, E), F32),
        pltpu.VMEM((S, PAIR, 128), BF),
        pltpu.VMEM((S, PAIR, 128), BF),
        pltpu.VMEM((S, PAIR, 128), BF),
        pltpu.VMEM((S, PAIR, 128), BF),
        pltpu.VMEM((TOK, E), BF),
        pltpu.VMEM((TOK, E), BF),
        pltpu.VMEM((NE, CORES, PAIR, W), BF),
        pltpu.VMEM((NQ, PAIR, W), BF),
        pltpu.VMEM((2, W, H), BF),
        pltpu.VMEM((2, W, H), BF),
        pltpu.VMEM((2, H, W), BF),
        dma((2, NQ)), dma((2, NQ)),
        dma((3,)), dma((3,)), dma((3,)),
        dma((2, ND)), dma((2, ND)),
        dma((3, NE)), dma((3, NE)),
        dma((ND,)), dma((ND,)),
        dma((4, 2, HZ)), dma((4, 2, HZ)),
        dma((4, 2, HZ)), dma((4, 2, HZ)),
        dma((S,)), dma((S,)),
        dma((S,)), dma((S,)),
        dma((NQ,)), dma((NQ,)),
        dma((3, 2)), dma((3, 2)),
    ]
    results = pl.pallas_call(
        functools.partial(kernel, sizes),
        out_shape=(
            pltpu.VMEM((TOK, W), BF),
            pltpu.VMEM((E, W), F32),
            pltpu.VMEM((local_count, W, H), BF),
            pltpu.VMEM((local_count, W, H), BF),
            pltpu.VMEM((local_count, H, W), BF),
        ),
        in_specs=[vmem] * 5 + [hbm] * 3,
        out_specs=(vmem, vmem, vmem, vmem, vmem),
        scratch_shapes=scratch,
        compiler_params=pltpu.CompilerParams(
            collective_id=0, has_side_effects=True, vmem_limit_bytes=56 * 1024 * 1024
        ),
        cost_estimate=pl.CostEstimate(
            flops=6 * 10**9, bytes_accessed=10**7, transcendentals=10**5
        ),
    )(tokens, cotangent, routing, w_router, running_mean, w_gate, w_up, w_down)
    grad_tokens, grad_router, *rest = results
    return (grad_tokens, grad_router.T, *rest)


def solution(mesh):
    return jax.shard_map(
        per_device,
        mesh=mesh,
        in_specs=(
            P("expert", "dp"),
            P("expert", "dp"),
            P("expert", None),
            P("dp", None),
            P(None, "dp"),
            P("expert", "dp", None),
            P("expert", "dp", None),
            P("expert", None, "dp"),
        ),
        out_specs=(
            P("expert", "dp"),
            P("dp", None),
            P("expert", "dp", None),
            P("expert", "dp", None),
            P("expert", None, "dp"),
        ),
        check_vma=False,
    )
```
